32 devices in a mesh: pool: 8 (over y, x, core), tp: 4 (over z).
Axes of the slice: x: 2, y: 2, z: 4, core: 2. Of those that a mesh axis runs over, the one named last changes fastest.
Arguments:
- turn_query: bfloat16 [4096, 2048], P('pool', 'tp'), may hold values from -16 to 16
- turn_key: bfloat16 [4096, 512], P('pool', 'tp'), may hold values from -16 to 16, as said below
- turn_value: bfloat16 [4096, 512], P('pool', 'tp'), may hold values from -6 to 6
- pool_keys: bfloat16 [512, 128, 512], P('pool', None, 'tp'), may hold values from -16 to 16, as said below
- pool_values: bfloat16 [512, 128, 512], P('pool', None, 'tp'), may hold values from -6 to 6
- seat_session: int32 [16], replicated, may hold values from 0 to 15, as said below
- history_len: int32 [16], replicated, may hold values from 1 to 4096, as said below
- block_map: int32 [16, 32], replicated, may hold values from 0 to 511, as said below
- out_weight: bfloat16 [2048, 8192], P('tp', 'pool'), may hold values from -0.1875 to 0.1875
Outputs:
- layer_out: bfloat16 [4096, 8192], P('pool', 'tp')
The draws below stay inside these ranges and needn't reach their ends.
Inputs may be any that keep to these rules, and one draw needn't show every extreme that they name: `seat_session`: A permutation of the sessions. `history_len`: the sessions of one owner, chosen afresh in every draw, have length 4096. Every slot of the pool is named exactly once. Call block j of session s live when j * 128 < history_len[s]; the slot's pool index is block_map[s, j] // 64. The live blocks of one pool index that belong to the sessions of one owner number at most 8; some owner receives exactly 8 from every pool index. `turn_key`: Real-valued keys. `pool_keys`: Real-valued keys; slots not named by a live block hold values that are never read.
All inputs are finite; a program needn't handle non-finite values.
Results may differ from the reference program's by a relative error of at most 0.019.
Values may be sent and summed in bfloat16 or wider, within the bound.
A program may use at most 128 MiB of HBM per device.

```python
import math
import jax
import jax.numpy as jnp
from jax import lax

D = 8192
HD = 128
QH_DEV = 4
NEW = 256
SESS_DEV = 2
BT = 128
MAXBLK = 32
QHEADS = 16
KVHEADS = 4
SESSIONS = 16
ROWS = 4096
HISTMAX = 4096
BLK_DEV = 64
SLOTS = 512
N_POOL = 8
N_TP = 4


def layout_ints(key):
    sub_keys = jax.random.split(key, 6)
    seating = jax.random.permutation(sub_keys[0], SESSIONS).astype(jnp.int32)
    first_len = jax.random.randint(sub_keys[1], (SESSIONS,), 0, HISTMAX, dtype=jnp.int32)
    second_len = jax.random.randint(sub_keys[2], (SESSIONS,), 0, HISTMAX, dtype=jnp.int32)
    lengths = jnp.minimum(first_len, second_len) + 1
    busiest = jax.random.randint(sub_keys[3], (), 0, N_POOL, dtype=jnp.int32)
    chosen = seating[busiest * SESS_DEV + jnp.arange(SESS_DEV, dtype=jnp.int32)]
    lengths = lengths.at[chosen].set(HISTMAX)
    orders = jax.vmap(lambda sub_key: jax.random.permutation(sub_key, MAXBLK))(jax.random.split(sub_keys[4], SESSIONS)).astype(jnp.int32)
    device_of = orders % N_POOL
    within = orders // N_POOL
    reserved = jnp.arange(SESSIONS, dtype=jnp.int32)[:, None] * (MAXBLK // N_POOL) + within
    shuffles = jax.vmap(lambda sub_key: jax.random.permutation(sub_key, BLK_DEV))(jax.random.split(sub_keys[5], N_POOL)).astype(jnp.int32)
    local_slot = shuffles[device_of, reserved]
    mapping = device_of * BLK_DEV + local_slot
    return (seating, lengths, mapping)


def draw_seat_session(key, part):
    seating, lengths, mapping = layout_ints(key)
    return seating


def draw_history_len(key, part):
    seating, lengths, mapping = layout_ints(key)
    return lengths


def draw_block_map(key, part):
    seating, lengths, mapping = layout_ints(key)
    return mapping


def draw_pool_keys(key, part):
    key = jax.random.fold_in(key, 11)
    sub_keys = jax.random.split(key, 2)
    shape = (SLOTS, BT, KVHEADS * HD)
    values = jax.random.truncated_normal(sub_keys[1], -6.0, 6.0, shape)
    return values.astype(jnp.bfloat16)


def draw_turn_key(key, part):
    key = jax.random.fold_in(key, 12)
    sub_keys = jax.random.split(key, 2)
    shape = (ROWS, KVHEADS * HD)
    values = jax.random.truncated_normal(sub_keys[1], -6.0, 6.0, shape)
    return values.astype(jnp.bfloat16)


def draw_turn_query(key, part):
    key = jax.random.fold_in(key, 13)
    sub_keys = jax.random.split(key, 2)
    shape = (ROWS, QHEADS * HD)
    values = jax.random.truncated_normal(sub_keys[1], -6.0, 6.0, shape)
    return values.astype(jnp.bfloat16)


def strengthened(drawn, stream_key, source, target, blocks, factor):
    owner, partner = [(jnp.arange(drawn.shape[dim]) // (drawn.shape[dim] // blocks)).reshape([-1 if axis == dim else 1 for axis in range(drawn.ndim)]) for dim in (source, target)]
    chosen = jax.random.permutation(stream_key, blocks)[partner]
    strong = (owner == chosen) | (owner == (partner + blocks // 2) % blocks)
    return jnp.where(strong, factor * drawn, drawn)


def levels(own_key, extent, cuts, low, top_value):
    loudness, own = 1.0, jax.random.fold_in(own_key, 6)
    for dim, blocks in cuts:
        steps = jnp.exp(jax.random.uniform(jax.random.fold_in(own, dim), (blocks,), jnp.float32, low / len(cuts), top_value / len(cuts)))
        loudness = loudness * jnp.repeat(steps, extent[dim] // blocks).reshape([-1 if axis == dim else 1 for axis in range(len(extent))])
    return loudness


def gaussian(own_key, dims, width, most, shards=(), kind=jnp.bfloat16):
    gain = levels(own_key, dims, shards, -0.22, 0.18) if shards else 1.0
    array = jax.random.normal(own_key, dims, jnp.float32) * width * gain
    return jnp.minimum(jnp.maximum(array, -most), most).astype(kind)


def heavy_noise(own_key, dims, width, most, shards, heavy, kind=jnp.bfloat16):
    drawn = width * jax.random.normal(own_key, dims, jnp.float32)
    if shards:
        drawn = drawn * levels(own_key, dims, shards, -0.22, 0.18)
    return jnp.clip(strengthened(drawn, jax.random.fold_in(own_key, 3), *heavy), -most, most).astype(kind)


def setup_inputs(seed: int = 0) -> dict:
    keys = jax.random.split(jax.random.key(seed), 10)
    turn_query = draw_turn_query(jax.random.fold_in(keys[9], 71), 0)
    turn_key = draw_turn_key(jax.random.fold_in(keys[9], 71), 0)
    turn_value = gaussian(keys[2], (ROWS, KVHEADS * HD), 1.0, 6.0, ((0, 8), (1, 4)))
    pool_keys = draw_pool_keys(jax.random.fold_in(keys[9], 71), 0)
    pool_values = gaussian(keys[4], (SLOTS, BT, KVHEADS * HD), 1.0, 6.0, ((0, 8), (2, 4)))
    seat_session = draw_seat_session(jax.random.fold_in(keys[9], 71), 0)
    history_len = draw_history_len(jax.random.fold_in(keys[9], 71), 0)
    block_map = draw_block_map(jax.random.fold_in(keys[9], 71), 0)
    out_weight = heavy_noise(keys[8], (QHEADS * HD, D), (QHEADS * HD) ** -0.5, 0.1875, ((0, 4), (1, 8)), (0, 1, 8, 2.0))
    return dict(turn_query=turn_query, turn_key=turn_key, turn_value=turn_value, pool_keys=pool_keys, pool_values=pool_values, seat_session=seat_session, history_len=history_len, block_map=block_map, out_weight=out_weight)


rope_base = 1000000.0

def rotate(values, positions):
    half_dim = values.shape[-1] // 2
    freq_index = jnp.arange(half_dim, dtype=jnp.float32)
    inverse = rope_base ** (-2.0 * freq_index / values.shape[-1])
    angles = positions.astype(jnp.float32)[:, None, None] * inverse[None, None, :]
    cosine = jnp.cos(angles)
    sine_part = jnp.sin(angles)
    lower_half = values[..., :half_dim]
    upper_half = values[..., half_dim:]
    return jnp.concatenate([lower_half * cosine - upper_half * sine_part, upper_half * cosine + lower_half * sine_part], axis=-1)

def narrow(values):
    return lax.optimization_barrier(values.astype(jnp.bfloat16))

def reference(turn_query, turn_key, turn_value, pool_keys, pool_values, seat_session, history_len, block_map, out_weight):
    scaling = 1.0 / math.sqrt(HD)

    def one_seat(seat_number):
        session = seat_session[seat_number]
        length = history_len[session]
        slot_ids = block_map[session]
        hist_keys = pool_keys[slot_ids].reshape(HISTMAX, KVHEADS, HD)
        hist_vals = pool_values[slot_ids].reshape(HISTMAX, KVHEADS, HD)
        row_start = (seat_number * NEW).astype(jnp.int32)
        queries = lax.dynamic_slice_in_dim(turn_query, row_start, NEW, 0).reshape(NEW, QHEADS, HD)
        new_keys = lax.dynamic_slice_in_dim(turn_key, row_start, NEW, 0).reshape(NEW, KVHEADS, HD)
        new_vals = lax.dynamic_slice_in_dim(turn_value, row_start, NEW, 0).reshape(NEW, KVHEADS, HD)
        turn_pos = length + jnp.arange(NEW, dtype=jnp.int32)
        hist_pos = jnp.arange(HISTMAX, dtype=jnp.int32)
        roped_query = narrow(rotate(queries.astype(jnp.float32), turn_pos))
        roped_keys = narrow(jnp.concatenate([rotate(hist_keys.astype(jnp.float32), hist_pos), rotate(new_keys.astype(jnp.float32), turn_pos)], axis=0))
        all_vals = jnp.concatenate([hist_vals, new_vals], axis=0)
        grouped = roped_query.reshape(NEW, KVHEADS, QH_DEV, HD)
        scores = jnp.einsum('tgqd,kgd->tgqk', grouped.astype(jnp.float32), roped_keys.astype(jnp.float32)) * scaling
        key_index = jnp.arange(HISTMAX + NEW, dtype=jnp.int32)[None, :]
        token_index = jnp.arange(NEW, dtype=jnp.int32)[:, None]
        visible = jnp.where(key_index < HISTMAX, key_index < length, key_index - HISTMAX <= token_index)
        scores = jnp.where(visible[:, None, None, :], scores, -jnp.inf)
        row_top = lax.optimization_barrier(jnp.max(scores, axis=-1, keepdims=True))
        weights = jnp.exp(scores - row_top)
        denominator = lax.optimization_barrier(jnp.sum(weights, axis=-1, keepdims=True))
        weighted = jnp.einsum('tgqk,kgd->tgqd', narrow(weights).astype(jnp.float32), all_vals.astype(jnp.float32))
        return (weighted / denominator).astype(jnp.bfloat16).reshape(NEW, QHEADS * HD)
    attended = lax.map(one_seat, jnp.arange(SESSIONS, dtype=jnp.int32)).reshape(ROWS, QHEADS * HD)
    running = jnp.zeros((ROWS, D), jnp.float32)
    width_group = QH_DEV * HD
    for group_number in range(N_TP):
        col_lo = group_number * width_group
        partial_value = jnp.dot(attended[:, col_lo:col_lo + width_group], out_weight[col_lo:col_lo + width_group], preferred_element_type=jnp.float32)
        running = running + narrow(partial_value).astype(jnp.float32)
    return running.astype(jnp.bfloat16)
```

```python
import functools
import math

import jax
import jax.numpy as jnp
import numpy as np
from jax import lax
from jax.experimental import pallas as pl
from jax.experimental.pallas import tpu as pltpu
from jax.sharding import PartitionSpec as P

rope_base = 1000000.0
MESH = pl.DeviceIdType.MESH
F32 = jnp.float32
BF16 = jnp.bfloat16
dot = functools.partial(jnp.dot, preferred_element_type=F32)


def kernel(
    pools,
    tps,
    seats,
    cap,
    meta_ref,
    tq_ref,
    tk_ref,
    tv_ref,
    cos_far,
    sin_far,
    cos_near,
    sin_near,
    send_k,
    send_v,
    weight,
    out_ref,
    keys,
    vals,
    gathered,
    attended,
    queries,
    scores,
    probs,
    flipped,
    acc,
    top,
    total,
    k_send,
    k_recv,
    v_send,
    v_recv,
    s_send,
    s_recv,
    g_send,
    g_recv,
    f_send,
    a_send,
    a_recv,
    local_sem,
):
    me = lax.axis_index("pool")
    row = lax.axis_index("tp")
    block = send_k.shape[1]
    head = send_k.shape[2]
    turn = tq_ref.shape[0] // seats
    group = tq_ref.shape[1] // head
    wide = group * turn
    chips = pools // 2
    share = pools // tps
    part = weight.shape[0] // pools
    w_cols = weight.shape[1]
    sibling = me + 1 - 2 * lax.rem(me, 2)
    core = lax.rem(me, 2)
    chip = me // 2
    target_row = me // share
    at_home = target_row == row

    barrier = pltpu.get_barrier_semaphore()

    def greet(pool_index, tp_index):
        pl.semaphore_signal(barrier, inc=1, device_id=(pool_index, tp_index), device_id_type=MESH)

    def greet_pool(i, carry):
        greet(lax.rem(me + i, pools), row)
        return carry

    lax.fori_loop(1, pools, greet_pool, 0)

    @pl.when(row > 0)
    def _():
        greet(me, row - 1)

    @pl.when(row < tps - 1)
    def _():
        greet(me, row + 1)

    def greet_source(i, carry):
        source_pool = row * share + i // tps
        source_row = lax.rem(i, tps)

        @pl.when(jnp.logical_not((source_pool == me) & (source_row == row)))
        def _():
            greet(source_pool, source_row)

        return carry

    lax.fori_loop(0, share * tps, greet_source, 0)
    greeted = (
        2 * pools
        - 1
        - at_home.astype(jnp.int32)
        + (row > 0).astype(jnp.int32)
        + (row < tps - 1).astype(jnp.int32)
    )
    pl.semaphore_wait(barrier, greeted)

    def kv_copies(q):
        rows = pl.ds(q * cap, cap)
        return (
            pltpu.make_async_remote_copy(
                src_ref=send_k.at[rows],
                dst_ref=keys.at[me],
                send_sem=k_send.at[q],
                recv_sem=k_recv.at[me],
                device_id=(q, row),
                device_id_type=MESH,
            ),
            pltpu.make_async_remote_copy(
                src_ref=send_v.at[rows],
                dst_ref=vals.at[me],
                send_sem=v_send.at[q],
                recv_sem=v_recv.at[me],
                device_id=(q, row),
                device_id_type=MESH,
            ),
        )

    def kv_arrival(s):
        return (
            pltpu.make_async_remote_copy(
                src_ref=keys.at[s],
                dst_ref=keys.at[s],
                send_sem=k_send.at[s],
                recv_sem=k_recv.at[s],
                device_id=(s, row),
                device_id_type=MESH,
            ),
            pltpu.make_async_remote_copy(
                src_ref=vals.at[s],
                dst_ref=vals.at[s],
                send_sem=v_send.at[s],
                recv_sem=v_recv.at[s],
                device_id=(s, row),
                device_id_type=MESH,
            ),
        )

    own_rows = pl.ds(me * cap, cap)
    own_k = pltpu.make_async_copy(send_k.at[own_rows], keys.at[me], local_sem.at[0])
    own_v = pltpu.make_async_copy(send_v.at[own_rows], vals.at[me], local_sem.at[1])
    own_k.start()
    own_v.start()

    def start_kv(i, carry):
        for copy in kv_copies(lax.rem(me + i, pools)):
            copy.start()
        return carry

    lax.fori_loop(1, pools, start_kv, 0)

    def scatter_copy(q):
        return pltpu.make_async_remote_copy(
            src_ref=weight.at[pl.ds(pl.multiple_of(q * part, part), part)],
            dst_ref=gathered.at[
                q,
                row,
                :,
                pl.ds(pl.multiple_of(lax.rem(me, share) * w_cols, w_cols), w_cols),
            ],
            send_sem=s_send.at[q],
            recv_sem=s_recv.at[lax.rem(me, share) * tps + row],
            device_id=(q, target_row),
            device_id_type=MESH,
        )

    own_w = pltpu.make_async_copy(
        weight.at[pl.ds(pl.multiple_of(me * part, part), part)],
        gathered.at[
            me, row, :, pl.ds(pl.multiple_of(lax.rem(me, share) * w_cols, w_cols), w_cols)
        ],
        local_sem.at[2],
    )

    def start_scatter(i, carry):
        q = lax.rem(me + i, pools)
        scatter_copy(q).start()
        return carry

    lax.fori_loop(1, pools, start_scatter, 0)

    @pl.when(at_home)
    def _():
        own_w.start()

    @pl.when(jnp.logical_not(at_home))
    def _():
        scatter_copy(me).start()

    def slab_copy(slab, pool_index, send_sem):
        return pltpu.make_async_remote_copy(
            src_ref=gathered.at[slab],
            dst_ref=gathered.at[slab],
            send_sem=send_sem,
            recv_sem=g_recv.at[slab],
            device_id=(pool_index, row),
            device_id_type=MESH,
        )

    def chip_peer(i):
        return lax.rem(chip + i, chips) * 2 + core

    def chip_source(i):
        return lax.rem(chip + chips - i, chips) * 2 + core

    def start_gather():
        def wait_piece(i, carry):
            piece_pool = row * share + i // tps
            piece_row = lax.rem(i, tps)

            @pl.when(jnp.logical_not((piece_pool == me) & (piece_row == row)))
            def _():
                landing = gathered.at[
                    me,
                    piece_row,
                    :,
                    pl.ds(pl.multiple_of((i // tps) * w_cols, w_cols), w_cols),
                ]
                pltpu.make_async_remote_copy(
                    src_ref=landing,
                    dst_ref=landing,
                    send_sem=s_send.at[0],
                    recv_sem=s_recv.at[i],
                    device_id=(piece_pool, piece_row),
                    device_id_type=MESH,
                ).wait_recv()

            return carry

        lax.fori_loop(0, share * tps, wait_piece, 0)

        @pl.when(at_home)
        def _():
            own_w.wait()

        def start_slab(i, carry):
            peer = chip_peer(i)
            slab_copy(me, peer, g_send.at[i]).start()
            return carry

        lax.fori_loop(1, chips, start_slab, 0)
        slab_copy(me, sibling, g_send.at[0]).start()

    def pass_on(i):
        slab = chip_source(i)
        copy = slab_copy(slab, sibling, f_send.at[i])
        copy.wait_recv()
        copy.start()

    factor = math.log2(math.e) / math.sqrt(head)
    tables = []
    for e in range(seats):
        far = cos_far.shape[0] - seats + e
        ca, sa = cos_far[far : far + 1, :], sin_far[far : far + 1, :]
        cb, sb = cos_near[...], sin_near[...]
        tables.append((ca * cb - sa * sb, sa * cb + ca * sb))

    def rope(x, cosine, sine):
        return x * cosine + pltpu.roll(x, head // 2, 1) * sine

    lanes = lax.broadcasted_iota(jnp.int32, (turn, wide), 1)
    unseen = lax.broadcasted_iota(jnp.int32, (turn, wide), 0) > lax.rem(lanes, turn)
    for e in range(seats):
        cosine, sine = tables[e]
        rows = slice(e * turn, (e + 1) * turn)
        for h in range(group):
            x = tq_ref[rows, h * head : (h + 1) * head].astype(F32)
            turned = rope(x, cosine, sine) * factor
            queries[e, :, h * turn : (h + 1) * turn] = turned.T.astype(BF16)
        new_keys = rope(tk_ref[rows, :].astype(F32), cosine, sine).astype(BF16)
        s = jnp.where(unseen, -jnp.inf, dot(new_keys, queries[e]))
        best = jnp.max(s, axis=0, keepdims=True)
        p = jnp.exp2(s - best)
        top[e : e + 1, :] = best
        total[e : e + 1, :] = jnp.sum(p, axis=0, keepdims=True)
        flipped_new = tv_ref[rows, :].astype(F32).T.astype(BF16)
        acc[e * head : (e + 1) * head, :] = dot(flipped_new, p.astype(BF16))

    depth = lax.broadcasted_iota(jnp.int32, (block, 1), 0)

    def attend(source):
        tops = [top[e : e + 1, :] for e in range(seats)]
        owners = []
        for b in range(cap):
            at = source * cap + b
            far, seat, limit = meta_ref[0, at], meta_ref[1, at], meta_ref[2, at]
            owners.append(seat)
            ca, sa = cos_far[pl.ds(far, 1), :], sin_far[pl.ds(far, 1), :]
            cb, sb = cos_near[0:block, :], sin_near[0:block, :]
            x = keys[source, b].astype(F32)
            turned = rope(x, ca * cb - sa * sb, sa * cb + ca * sb).astype(BF16)
            s = jnp.where(depth < limit, dot(turned, queries[seat]), -jnp.inf)
            scores[b * block : (b + 1) * block, :] = s
            best = jnp.max(s, axis=0, keepdims=True)
            upright = vals[source, b].astype(F32).T
            for e in range(seats):
                tops[e] = jnp.maximum(tops[e], jnp.where(seat == e, best, -jnp.inf))
                flipped[e * head : (e + 1) * head, b * block : (b + 1) * block] = jnp.where(
                    seat == e, upright, 0.0
                ).astype(BF16)
        alphas = [jnp.exp2(top[e : e + 1, :] - tops[e]) for e in range(seats)]
        sums = [total[e : e + 1, :] * alphas[e] for e in range(seats)]
        for b in range(cap):
            span = slice(b * block, (b + 1) * block)
            base = tops[0]
            for e in range(1, seats):
                base = jnp.where(owners[b] == e, tops[e], base)
            p = jnp.exp2(scores[span, :] - base)
            added = jnp.sum(p, axis=0, keepdims=True)
            for e in range(seats):
                sums[e] = sums[e] + jnp.where(owners[b] == e, added, 0.0)
            probs[span, :] = p.astype(BF16)
        gained = dot(flipped[...], probs[...])
        for e in range(seats):
            rows = slice(e * head, (e + 1) * head)
            acc[rows, :] = acc[rows, :] * alphas[e] + gained[rows, :]
            top[e : e + 1, :] = tops[e]
            total[e : e + 1, :] = sums[e]

    def step(i, carry):
        source = lax.rem(me + pools - i, pools)

        @pl.when(i == 0)
        def _():
            own_k.wait()
            own_v.wait()

        @pl.when(i > 0)
        def _():
            for copy in kv_arrival(source):
                copy.wait_recv()

        @pl.when(i == pools - 2)
        def _():
            start_gather()

        attend(source)
        return carry

    lax.fori_loop(0, pools, step, 0)

    for e in range(seats):
        rows = slice(e * turn, (e + 1) * turn)
        final = acc[e * head : (e + 1) * head, :] / total[e : e + 1, :]
        for h in range(group):
            attended[row, rows, h * head : (h + 1) * head] = (
                final[:, h * turn : (h + 1) * turn].T.astype(BF16)
            )

    def slot_copy(slot, neighbour, way, hop):
        return pltpu.make_async_remote_copy(
            src_ref=attended.at[slot],
            dst_ref=attended.at[slot],
            send_sem=a_send.at[way, hop],
            recv_sem=a_recv.at[slot],
            device_id=(me, neighbour),
            device_id_type=MESH,
        )

    def hop_sends(hop, act):
        @pl.when((row - hop >= 0) & (row < tps - 1))
        def _():
            act(slot_copy(row - hop, row + 1, 0, hop))

        @pl.when((row + hop < tps) & (row > 0))
        def _():
            act(slot_copy(row + hop, row - 1, 1, hop))

    def hop_waits(hop):
        @pl.when(row - hop >= 0)
        def _():
            slot_copy(row - hop, row - 1, 0, 0).wait_recv()

        @pl.when(row + hop < tps)
        def _():
            slot_copy(row + hop, row + 1, 1, 0).wait_recv()

    hop_sends(0, lambda copy: copy.start())
    passed = 1
    for hop in range(1, tps):
        hop_waits(hop)
        if hop < tps - 1:
            hop_sends(hop, lambda copy: copy.start())
        if passed < chips:
            pass_on(passed)
            passed += 1

    def rest(i, carry):
        pass_on(i)
        return carry

    lax.fori_loop(passed, chips, rest, 0)

    slab_copy(sibling, sibling, g_send.at[0]).wait_recv()

    def wait_passed(i, carry):
        slab = chip_source(i) - core + lax.rem(sibling, 2)
        slab_copy(slab, sibling, g_send.at[0]).wait_recv()
        return carry

    lax.fori_loop(1, chips, wait_passed, 0)

    tile = 256

    def project(n, carry):
        cols = pl.ds(pl.multiple_of(n * tile, tile), tile)
        result = jnp.zeros((out_ref.shape[0], tile), F32)
        for t in range(tps):
            w = gathered[:, t, :, cols].reshape(pools * part, tile)
            result = result + dot(attended[t], w)
        out_ref[:, cols] = result.astype(BF16)
        return carry

    lax.fori_loop(0, out_ref.shape[1] // tile, project, 0)

    def wait_sends(i, carry):
        q = lax.rem(me + i, pools)
        for copy in kv_copies(q):
            copy.wait_send()
        scatter_copy(q).wait_send()
        return carry

    lax.fori_loop(1, pools, wait_sends, 0)

    @pl.when(jnp.logical_not(at_home))
    def _():
        scatter_copy(me).wait_send()

    def wait_slabs(i, carry):
        slab_copy(me, chip_peer(i), g_send.at[i]).wait_send()
        slab_copy(chip_source(i), sibling, f_send.at[i]).wait_send()
        return carry

    lax.fori_loop(1, chips, wait_slabs, 0)
    slab_copy(me, sibling, g_send.at[0]).wait_send()
    for hop in range(tps - 1):
        hop_sends(hop, lambda copy: copy.wait_send())


def local(
    turn_query,
    turn_key,
    turn_value,
    pool_keys,
    pool_values,
    seat_session,
    history_len,
    block_map,
    out_weight,
):
    pools = lax.axis_size("pool")
    tps = lax.axis_size("tp")
    me = lax.axis_index("pool")
    blocks_here, block, head = pool_keys.shape
    block_count = block_map.shape[1]
    seats = seat_session.shape[0] // pools
    cap = seats * block_count // pools
    count = seats * block_count
    rows, width = turn_query.shape
    turn = rows // seats
    group = width // head
    wide = group * turn
    part = out_weight.shape[0] // pools
    out_cols = out_weight.shape[1] * pools // tps

    seat_length = history_len[seat_session]
    seat_map = block_map[seat_session]
    home = (seat_map // blocks_here).reshape(pools, count)
    slot = (seat_map % blocks_here).reshape(pools, count)
    numbers = jnp.arange(block_count, dtype=jnp.int32)
    alive = (numbers[None, :] * block < seat_length[:, None]).reshape(pools, count)
    ranks = jnp.arange(cap, dtype=jnp.int32)
    leaving = alive & (home == me)
    send_rank = jnp.cumsum(leaving.astype(jnp.int32), axis=1) - 1
    chosen = leaving[:, None, :] & (send_rank[:, None, :] == ranks[None, :, None])
    slot_table = jnp.sum(jnp.where(chosen, slot[:, None, :], 0), axis=2).reshape(pools * cap)
    send_keys = pool_keys[slot_table]
    send_vals = pool_values[slot_table]

    own_home = lax.dynamic_slice_in_dim(home, me, 1, 0)
    own_alive = lax.dynamic_slice_in_dim(alive, me, 1, 0)
    own_lengths = lax.dynamic_slice_in_dim(seat_length, me * seats, seats, 0)
    coming = own_alive & (own_home == jnp.arange(pools, dtype=jnp.int32)[:, None])
    coming_rank = jnp.cumsum(coming.astype(jnp.int32), axis=1) - 1
    landed = coming[:, None, :] & (coming_rank[:, None, :] == ranks[None, :, None])
    landed = landed.reshape(pools * cap, count)
    entry_number = jnp.tile(numbers, seats)
    entry_seat = jnp.repeat(jnp.arange(seats, dtype=jnp.int32), block_count)
    entry_limit = jnp.repeat(own_lengths, block_count) - entry_number * block
    meta = jnp.stack(
        [
            jnp.sum(jnp.where(landed, entry[None, :], 0), axis=1)
            for entry in (entry_number, entry_seat, entry_limit)
        ]
    )

    half = head // 2
    inverse = rope_base ** (-2.0 * np.arange(half) / head)
    inverse = np.concatenate([inverse, inverse])
    signs = np.concatenate([-np.ones(half), np.ones(half)])
    near = np.arange(turn)[:, None] * inverse[None, :]
    far = (np.arange(block_count) * block)[:, None] * inverse[None, :]
    cos_near = jnp.asarray(np.cos(near), F32)
    sin_near = jnp.asarray(np.sin(near) * signs, F32)
    start = own_lengths.astype(F32)[:, None] * jnp.asarray(inverse, F32)[None, :]
    cos_far = jnp.concatenate([jnp.asarray(np.cos(far), F32), jnp.cos(start)], axis=0)
    sin_far = jnp.concatenate(
        [jnp.asarray(np.sin(far) * signs, F32), jnp.sin(start) * jnp.asarray(signs, F32)], axis=0
    )

    in_vmem = pl.BlockSpec(memory_space=pltpu.VMEM)
    anywhere = pl.BlockSpec(memory_space=pl.ANY)
    dma = pltpu.SemaphoreType.DMA
    chips = pools // 2
    return pl.pallas_call(
        functools.partial(kernel, pools, tps, seats, cap),
        out_shape=jax.ShapeDtypeStruct((rows, out_cols), BF16),
        in_specs=[pl.BlockSpec(memory_space=pltpu.SMEM)] + [in_vmem] * 7 + [anywhere] * 3,
        out_specs=in_vmem,
        scratch_shapes=[
            pltpu.VMEM((pools, cap, block, head), BF16),
            pltpu.VMEM((pools, cap, block, head), BF16),
            pltpu.VMEM((pools, tps, part, out_cols), BF16),
            pltpu.VMEM((tps, rows, width), BF16),
            pltpu.VMEM((seats, head, wide), BF16),
            pltpu.VMEM((cap * block, wide), F32),
            pltpu.VMEM((cap * block, wide), BF16),
            pltpu.VMEM((seats * head, cap * block), BF16),
            pltpu.VMEM((seats * head, wide), F32),
            pltpu.VMEM((seats, wide), F32),
            pltpu.VMEM((seats, wide), F32),
            dma((pools,)),
            dma((pools,)),
            dma((pools,)),
            dma((pools,)),
            dma((pools,)),
            dma((pools,)),
            dma((chips,)),
            dma((pools,)),
            dma((chips,)),
            dma((2, tps)),
            dma((tps,)),
            dma((3,)),
        ],
        compiler_params=pltpu.CompilerParams(
            collective_id=0, has_side_effects=True, vmem_limit_bytes=56 * 1024 * 1024
        ),
    )(
        meta,
        turn_query,
        turn_key,
        turn_value,
        cos_far,
        sin_far,
        cos_near,
        sin_near,
        send_keys,
        send_vals,
        out_weight,
    )


def solution(mesh):
    return jax.shard_map(
        local,
        mesh=mesh,
        in_specs=(
            P("pool", "tp"),
            P("pool", "tp"),
            P("pool", "tp"),
            P("pool", None, "tp"),
            P("pool", None, "tp"),
            P(),
            P(),
            P(),
            P("tp", "pool"),
        ),
        out_specs=P("pool", "tp"),
        check_vma=False,
    )
```

```python
import functools
import math

import jax
import jax.numpy as jnp
import numpy as np
from jax import lax
from jax.experimental import pallas as pl
from jax.experimental.pallas import tpu as pltpu
from jax.sharding import PartitionSpec as P

rope_base = 1000000.0
MESH = pl.DeviceIdType.MESH
F32 = jnp.float32
BF16 = jnp.bfloat16
dot = functools.partial(jnp.dot, preferred_element_type=F32)


def kernel(
    pools,
    tps,
    seats,
    cap,
    meta_ref,
    tq_ref,
    tk_ref,
    tv_ref,
    cos_far,
    sin_far,
    cos_near,
    sin_near,
    send_k,
    send_v,
    weight,
    out_ref,
    keys,
    vals,
    gathered,
    attended,
    queries,
    wide_keys,
    scores,
    probs,
    flipped,
    acc,
    top,
    total,
    k_send,
    k_recv,
    v_send,
    v_recv,
    s_send,
    s_recv,
    g_send,
    g_recv,
    f_send,
    a_send,
    a_recv,
    local_sem,
):
    me = lax.axis_index("pool")
    row = lax.axis_index("tp")
    block = send_k.shape[1]
    head = send_k.shape[2]
    turn = tq_ref.shape[0] // seats
    group = tq_ref.shape[1] // head
    wide = group * turn
    chips = pools // 2
    share = pools // tps
    part = weight.shape[0] // pools
    w_cols = weight.shape[1]
    sibling = me + 1 - 2 * lax.rem(me, 2)
    core = lax.rem(me, 2)
    chip = me // 2
    target_row = me // share
    at_home = target_row == row

    barrier = pltpu.get_barrier_semaphore()

    def greet(pool_index, tp_index):
        pl.semaphore_signal(barrier, inc=1, device_id=(pool_index, tp_index), device_id_type=MESH)

    def greet_pool(i, carry):
        greet(lax.rem(me + i, pools), row)
        return carry

    lax.fori_loop(1, pools, greet_pool, 0)

    @pl.when(row > 0)
    def _():
        greet(me, row - 1)

    @pl.when(row < tps - 1)
    def _():
        greet(me, row + 1)

    def greet_source(i, carry):
        source_pool = row * share + i // tps
        source_row = lax.rem(i, tps)

        @pl.when(jnp.logical_not((source_pool == me) & (source_row == row)))
        def _():
            greet(source_pool, source_row)

        return carry

    lax.fori_loop(0, share * tps, greet_source, 0)
    greeted = (
        2 * pools
        - 1
        - at_home.astype(jnp.int32)
        + (row > 0).astype(jnp.int32)
        + (row < tps - 1).astype(jnp.int32)
    )
    pl.semaphore_wait(barrier, greeted)

    def kv_copies(q):
        rows = pl.ds(q * cap, cap)
        return (
            pltpu.make_async_remote_copy(
                src_ref=send_k.at[rows],
                dst_ref=keys.at[me],
                send_sem=k_send.at[q],
                recv_sem=k_recv.at[me],
                device_id=(q, row),
                device_id_type=MESH,
            ),
            pltpu.make_async_remote_copy(
                src_ref=send_v.at[rows],
                dst_ref=vals.at[me],
                send_sem=v_send.at[q],
                recv_sem=v_recv.at[me],
                device_id=(q, row),
                device_id_type=MESH,
            ),
        )

    def kv_arrival(s):
        return (
            pltpu.make_async_remote_copy(
                src_ref=keys.at[s],
                dst_ref=keys.at[s],
                send_sem=k_send.at[s],
                recv_sem=k_recv.at[s],
                device_id=(s, row),
                device_id_type=MESH,
            ),
            pltpu.make_async_remote_copy(
                src_ref=vals.at[s],
                dst_ref=vals.at[s],
                send_sem=v_send.at[s],
                recv_sem=v_recv.at[s],
                device_id=(s, row),
                device_id_type=MESH,
            ),
        )

    def scatter_copy(q):
        return pltpu.make_async_remote_copy(
            src_ref=weight.at[pl.ds(pl.multiple_of(q * part, part), part)],
            dst_ref=gathered.at[
                q,
                row,
                :,
                pl.ds(pl.multiple_of(lax.rem(me, share) * w_cols, w_cols), w_cols),
            ],
            send_sem=s_send.at[q],
            recv_sem=s_recv.at[lax.rem(me, share) * tps + row],
            device_id=(q, target_row),
            device_id_type=MESH,
        )

    own_w = pltpu.make_async_copy(
        weight.at[pl.ds(pl.multiple_of(me * part, part), part)],
        gathered.at[
            me, row, :, pl.ds(pl.multiple_of(lax.rem(me, share) * w_cols, w_cols), w_cols)
        ],
        local_sem.at[2],
    )

    def start_scatter(i, carry):
        q = lax.rem(me + i, pools)
        scatter_copy(q).start()
        return carry

    lax.fori_loop(1, pools, start_scatter, 0)

    @pl.when(at_home)
    def _():
        own_w.start()

    @pl.when(jnp.logical_not(at_home))
    def _():
        scatter_copy(me).start()

    own_rows = pl.ds(me * cap, cap)
    own_k = pltpu.make_async_copy(send_k.at[own_rows], keys.at[me], local_sem.at[0])
    own_v = pltpu.make_async_copy(send_v.at[own_rows], vals.at[me], local_sem.at[1])
    own_k.start()
    own_v.start()

    def start_kv(i, carry):
        for copy in kv_copies(lax.rem(me + i, pools)):
            copy.start()
        return carry

    lax.fori_loop(1, pools, start_kv, 0)

    def slab_copy(slab, pool_index, send_sem):
        return pltpu.make_async_remote_copy(
            src_ref=gathered.at[slab],
            dst_ref=gathered.at[slab],
            send_sem=send_sem,
            recv_sem=g_recv.at[slab],
            device_id=(pool_index, row),
            device_id_type=MESH,
        )

    def chip_peer(i):
        return lax.rem(chip + i, chips) * 2 + core

    def chip_source(i):
        return lax.rem(chip + chips - i, chips) * 2 + core

    def start_gather():
        def wait_piece(i, carry):
            piece_pool = row * share + i // tps
            piece_row = lax.rem(i, tps)

            @pl.when(jnp.logical_not((piece_pool == me) & (piece_row == row)))
            def _():
                landing = gathered.at[
                    me,
                    piece_row,
                    :,
                    pl.ds(pl.multiple_of((i // tps) * w_cols, w_cols), w_cols),
                ]
                pltpu.make_async_remote_copy(
                    src_ref=landing,
                    dst_ref=landing,
                    send_sem=s_send.at[0],
                    recv_sem=s_recv.at[i],
                    device_id=(piece_pool, piece_row),
                    device_id_type=MESH,
                ).wait_recv()

            return carry

        lax.fori_loop(0, share * tps, wait_piece, 0)

        @pl.when(at_home)
        def _():
            own_w.wait()

        def start_slab(i, carry):
            peer = chip_peer(i)
            slab_copy(me, peer, g_send.at[i]).start()
            return carry

        lax.fori_loop(1, chips, start_slab, 0)
        slab_copy(me, sibling, g_send.at[0]).start()

    def pass_on(i):
        slab = chip_source(i)
        copy = slab_copy(slab, sibling, f_send.at[i])
        copy.wait_recv()
        copy.start()

    factor = math.log2(math.e) / math.sqrt(head)
    tables = []
    for e in range(seats):
        far, near = meta_ref[0, pools * cap + e], meta_ref[1, pools * cap + e]
        ca, sa = cos_far[pl.ds(far, 1), :], sin_far[pl.ds(far, 1), :]
        cb, sb = cos_near[pl.ds(near, 1), :], sin_near[pl.ds(near, 1), :]
        ca, sa = ca * cb - sa * sb, sa * cb + ca * sb
        cb, sb = cos_near[...], sin_near[...]
        tables.append((ca * cb - sa * sb, sa * cb + ca * sb))

    def rope(x, cosine, sine):
        return x * cosine + pltpu.roll(x, head // 2, 1) * sine

    lanes = lax.broadcasted_iota(jnp.int32, (turn, wide), 1)
    unseen = lax.broadcasted_iota(jnp.int32, (turn, wide), 0) > lax.rem(lanes, turn)
    for e in range(seats):
        cosine, sine = tables[e]
        rows = slice(e * turn, (e + 1) * turn)
        for h in range(group):
            x = tq_ref[rows, h * head : (h + 1) * head].astype(F32)
            turned = rope(x, cosine, sine) * factor
            queries[e * head : (e + 1) * head, h * turn : (h + 1) * turn] = turned.T.astype(BF16)
        new_keys = rope(tk_ref[rows, :].astype(F32), cosine, sine).astype(BF16)
        s = jnp.where(unseen, -jnp.inf, dot(new_keys, queries[e * head : (e + 1) * head, :]))
        best = jnp.max(s, axis=0, keepdims=True)
        p = jnp.exp2(s - best)
        top[e : e + 1, :] = best
        total[e : e + 1, :] = jnp.sum(p, axis=0, keepdims=True)
        flipped_new = tv_ref[rows, :].astype(F32).T.astype(BF16)
        acc[e * head : (e + 1) * head, :] = dot(flipped_new, p.astype(BF16))

    depth = lax.broadcasted_iota(jnp.int32, (block, 1), 0)

    def attend(source):
        tops = [top[e : e + 1, :] for e in range(seats)]
        owners = []
        for b in range(cap):
            at = source * cap + b
            far, seat = meta_ref[0, at], meta_ref[1, at]
            owners.append(seat)
            ca, sa = cos_far[pl.ds(far, 1), :], sin_far[pl.ds(far, 1), :]
            cb, sb = cos_near[0:block, :], sin_near[0:block, :]
            x = keys[source, b].astype(F32)
            turned = rope(x, ca * cb - sa * sb, sa * cb + ca * sb)
            upright = vals[source, b].astype(F32).T
            span = slice(b * block, (b + 1) * block)
            for e in range(seats):
                part_e = slice(e * head, (e + 1) * head)
                wide_keys[span, part_e] = jnp.where(seat == e, turned, 0.0).astype(BF16)
                flipped[part_e, span] = jnp.where(seat == e, upright, 0.0).astype(BF16)
        run = math.gcd(cap, 4)
        for first in range(0, cap, run):
            several = dot(
                wide_keys[first * block : (first + run) * block, :], queries[...]
            )
            for b in range(first, first + run):
                s = several[(b - first) * block : (b - first + 1) * block, :]
                s = jnp.where(depth < meta_ref[2, source * cap + b], s, -jnp.inf)
                scores[b * block : (b + 1) * block, :] = s
                best = jnp.max(s, axis=0, keepdims=True)
                for e in range(seats):
                    tops[e] = jnp.maximum(tops[e], jnp.where(owners[b] == e, best, -jnp.inf))
        alphas = [jnp.exp2(top[e : e + 1, :] - tops[e]) for e in range(seats)]
        sums = [total[e : e + 1, :] * alphas[e] for e in range(seats)]
        for b in range(cap):
            span = slice(b * block, (b + 1) * block)
            base = tops[0]
            for e in range(1, seats):
                base = jnp.where(owners[b] == e, tops[e], base)
            p = jnp.exp2(scores[span, :] - base)
            added = jnp.sum(p, axis=0, keepdims=True)
            for e in range(seats):
                sums[e] = sums[e] + jnp.where(owners[b] == e, added, 0.0)
            probs[span, :] = p.astype(BF16)
        gained = dot(flipped[...], probs[...])
        for e in range(seats):
            rows = slice(e * head, (e + 1) * head)
            acc[rows, :] = acc[rows, :] * alphas[e] + gained[rows, :]
            top[e : e + 1, :] = tops[e]
            total[e : e + 1, :] = sums[e]

    def step(i, carry):
        source = lax.rem(me + pools - i, pools)

        @pl.when(i == 0)
        def _():
            own_k.wait()
            own_v.wait()

        @pl.when(i > 0)
        def _():
            for copy in kv_arrival(source):
                copy.wait_recv()

        @pl.when(i == pools - 3)
        def _():
            start_gather()

        attend(source)
        return carry

    lax.fori_loop(0, pools, step, 0)

    for e in range(seats):
        rows = slice(e * turn, (e + 1) * turn)
        final = acc[e * head : (e + 1) * head, :] / total[e : e + 1, :]
        for h in range(group):
            attended[row, rows, h * head : (h + 1) * head] = (
                final[:, h * turn : (h + 1) * turn].T.astype(BF16)
            )

    def slot_copy(slot, neighbour, way, hop):
        return pltpu.make_async_remote_copy(
            src_ref=attended.at[slot],
            dst_ref=attended.at[slot],
            send_sem=a_send.at[way, hop],
            recv_sem=a_recv.at[slot],
            device_id=(me, neighbour),
            device_id_type=MESH,
        )

    def hop_sends(hop, act):
        @pl.when((row - hop >= 0) & (row < tps - 1))
        def _():
            act(slot_copy(row - hop, row + 1, 0, hop))

        @pl.when((row + hop < tps) & (row > 0))
        def _():
            act(slot_copy(row + hop, row - 1, 1, hop))

    def hop_waits(hop):
        @pl.when(row - hop >= 0)
        def _():
            slot_copy(row - hop, row - 1, 0, 0).wait_recv()

        @pl.when(row + hop < tps)
        def _():
            slot_copy(row + hop, row + 1, 1, 0).wait_recv()

    hop_sends(0, lambda copy: copy.start())
    passed = 1
    for hop in range(1, tps):
        hop_waits(hop)
        if hop < tps - 1:
            hop_sends(hop, lambda copy: copy.start())
        if passed < chips:
            pass_on(passed)
            passed += 1

    def rest(i, carry):
        pass_on(i)
        return carry

    lax.fori_loop(passed, chips, rest, 0)

    slab_copy(sibling, sibling, g_send.at[0]).wait_recv()

    def wait_passed(i, carry):
        slab = chip_source(i) - core + lax.rem(sibling, 2)
        slab_copy(slab, sibling, g_send.at[0]).wait_recv()
        return carry

    lax.fori_loop(1, chips, wait_passed, 0)

    tile = 256

    def project(n, carry):
        cols = pl.ds(pl.multiple_of(n * tile, tile), tile)
        result = jnp.zeros((out_ref.shape[0], tile), F32)
        for t in range(tps):
            w = gathered[:, t, :, cols].reshape(pools * part, tile)
            result = result + dot(attended[t], w)
        out_ref[:, cols] = result.astype(BF16)
        return carry

    lax.fori_loop(0, out_ref.shape[1] // tile, project, 0)

    def wait_sends(i, carry):
        q = lax.rem(me + i, pools)
        for copy in kv_copies(q):
            copy.wait_send()
        scatter_copy(q).wait_send()
        return carry

    lax.fori_loop(1, pools, wait_sends, 0)

    @pl.when(jnp.logical_not(at_home))
    def _():
        scatter_copy(me).wait_send()

    def wait_slabs(i, carry):
        slab_copy(me, chip_peer(i), g_send.at[i]).wait_send()
        slab_copy(chip_source(i), sibling, f_send.at[i]).wait_send()
        return carry

    lax.fori_loop(1, chips, wait_slabs, 0)
    slab_copy(me, sibling, g_send.at[0]).wait_send()
    for hop in range(tps - 1):
        hop_sends(hop, lambda copy: copy.wait_send())


def pack(
    pools,
    seats,
    cap,
    seat_ref,
    len_ref,
    map_ref,
    pool_k,
    pool_v,
    send_k,
    send_v,
    meta_ref,
    counts,
    arrivals,
    k_sem,
    v_sem,
):
    me = lax.axis_index("pool")
    blocks_here, block = pool_k.shape[0], pool_k.shape[1]

    def live_blocks(seat):
        session = seat_ref[seat]
        length = len_ref[session]
        return session, length, lax.div(length + (block - 1), block)

    def copies(slot, at):
        return (
            pltpu.make_async_copy(pool_k.at[slot], send_k.at[at], k_sem.at[at]),
            pltpu.make_async_copy(pool_v.at[slot], send_v.at[at], v_sem.at[at]),
        )

    def owner_blocks(owner, carry):
        rank = jnp.int32(0)
        for e in range(seats):
            session, _, live = live_blocks(owner * seats + e)

            def one(j, rank):
                slot = map_ref[session, j]
                here = lax.div(slot, blocks_here) == me

                @pl.when(here)
                def _():
                    for copy in copies(lax.rem(slot, blocks_here), owner * cap + rank):
                        copy.start()

                return rank + here.astype(jnp.int32)

            rank = lax.fori_loop(0, live, one, rank)
        counts[owner] = rank
        return carry

    lax.fori_loop(0, pools, owner_blocks, 0)

    def clear(at, carry):
        meta_ref[0, at] = 0
        meta_ref[1, at] = -1
        meta_ref[2, at] = 0
        return carry

    lax.fori_loop(0, pools * cap + seats, clear, 0)

    def reset(source, carry):
        arrivals[source] = 0
        return carry

    lax.fori_loop(0, pools, reset, 0)

    for e in range(seats):
        session, length, live = live_blocks(me * seats + e)

        def arriving(j, carry):
            source = lax.div(map_ref[session, j], blocks_here)
            rank = arrivals[source]
            arrivals[source] = rank + 1
            at = source * cap + rank
            meta_ref[0, at] = j
            meta_ref[1, at] = e
            meta_ref[2, at] = length - j * block
            return carry

        lax.fori_loop(0, live, arriving, 0)
        meta_ref[0, pools * cap + e] = lax.div(length, block)
        meta_ref[1, pools * cap + e] = lax.rem(length, block)

    def wait_owner(owner, carry):
        def one(rank, carry):
            for copy in copies(0, owner * cap + rank):
                copy.wait()
            return carry

        lax.fori_loop(0, counts[owner], one, 0)
        return carry

    lax.fori_loop(0, pools, wait_owner, 0)


def local(
    turn_query,
    turn_key,
    turn_value,
    pool_keys,
    pool_values,
    seat_session,
    history_len,
    block_map,
    out_weight,
):
    pools = lax.axis_size("pool")
    tps = lax.axis_size("tp")
    block, head = pool_keys.shape[1:]
    block_count = block_map.shape[1]
    seats = seat_session.shape[0] // pools
    cap = seats * block_count // pools
    rows, width = turn_query.shape
    turn = rows // seats
    group = width // head
    wide = group * turn
    part = out_weight.shape[0] // pools
    out_cols = out_weight.shape[1] * pools // tps

    in_vmem = pl.BlockSpec(memory_space=pltpu.VMEM)
    in_smem = pl.BlockSpec(memory_space=pltpu.SMEM)
    anywhere = pl.BlockSpec(memory_space=pl.ANY)
    dma = pltpu.SemaphoreType.DMA

    blocks = jax.ShapeDtypeStruct((pools * cap, block, head), BF16)
    send_keys, send_vals, meta = pl.pallas_call(
        functools.partial(pack, pools, seats, cap),
        out_shape=(blocks, blocks, jax.ShapeDtypeStruct((3, pools * cap + seats), jnp.int32)),
        in_specs=[in_smem] * 3 + [anywhere] * 2,
        out_specs=(anywhere, anywhere, in_smem),
        scratch_shapes=[
            pltpu.SMEM((pools,), jnp.int32),
            pltpu.SMEM((pools,), jnp.int32),
            dma((pools * cap,)),
            dma((pools * cap,)),
        ],
    )(seat_session, history_len, block_map, pool_keys, pool_values)

    half = head // 2
    inverse = rope_base ** (-2.0 * np.arange(half) / head)
    inverse = np.concatenate([inverse, inverse])
    signs = np.concatenate([-np.ones(half), np.ones(half)])
    near = np.arange(turn)[:, None] * inverse[None, :]
    far = (np.arange(block_count + 1) * block)[:, None] * inverse[None, :]
    cos_near = jnp.asarray(np.cos(near), F32)
    sin_near = jnp.asarray(np.sin(near) * signs, F32)
    cos_far = jnp.asarray(np.cos(far), F32)
    sin_far = jnp.asarray(np.sin(far) * signs, F32)

    chips = pools // 2
    return pl.pallas_call(
        functools.partial(kernel, pools, tps, seats, cap),
        out_shape=jax.ShapeDtypeStruct((rows, out_cols), BF16),
        in_specs=[in_smem] + [in_vmem] * 7 + [anywhere] * 3,
        out_specs=in_vmem,
        scratch_shapes=[
            pltpu.VMEM((pools, cap, block, head), BF16),
            pltpu.VMEM((pools, cap, block, head), BF16),
            pltpu.VMEM((pools, tps, part, out_cols), BF16),
            pltpu.VMEM((tps, rows, width), BF16),
            pltpu.VMEM((seats * head, wide), BF16),
            pltpu.VMEM((cap * block, seats * head), BF16),
            pltpu.VMEM((cap * block, wide), F32),
            pltpu.VMEM((cap * block, wide), BF16),
            pltpu.VMEM((seats * head, cap * block), BF16),
            pltpu.VMEM((seats * head, wide), F32),
            pltpu.VMEM((seats, wide), F32),
            pltpu.VMEM((seats, wide), F32),
            dma((pools,)),
            dma((pools,)),
            dma((pools,)),
            dma((pools,)),
            dma((pools,)),
            dma((pools,)),
            dma((chips,)),
            dma((pools,)),
            dma((chips,)),
            dma((2, tps)),
            dma((tps,)),
            dma((3,)),
        ],
        compiler_params=pltpu.CompilerParams(
            collective_id=0, has_side_effects=True, vmem_limit_bytes=56 * 1024 * 1024
        ),
    )(
        meta,
        turn_query,
        turn_key,
        turn_value,
        cos_far,
        sin_far,
        cos_near,
        sin_near,
        send_keys,
        send_vals,
        out_weight,
    )


def solution(mesh):
    return jax.shard_map(
        local,
        mesh=mesh,
        in_specs=(
            P("pool", "tp"),
            P("pool", "tp"),
            P("pool", "tp"),
            P("pool", None, "tp"),
            P("pool", None, "tp"),
            P(),
            P(),
            P(),
            P("tp", "pool"),
        ),
        out_specs=P("pool", "tp"),
        check_vma=False,
    )
```

```python
import functools
import math

import jax
import jax.numpy as jnp
import numpy as np
from jax import lax
from jax.experimental import pallas as pl
from jax.experimental.pallas import tpu as pltpu
from jax.sharding import PartitionSpec as P

rope_base = 1000000.0
MESH = pl.DeviceIdType.MESH
F32 = jnp.float32
BF16 = jnp.bfloat16
dot = functools.partial(jnp.dot, preferred_element_type=F32)


def kernel(
    pools,
    tps,
    seats,
    cap,
    meta_ref,
    tq_ref,
    tk_ref,
    tv_ref,
    cos_far,
    sin_far,
    cos_near,
    sin_near,
    pool_k,
    pool_v,
    weight,
    out_ref,
    send_k,
    send_v,
    keys,
    vals,
    gathered,
    attended,
    queries,
    wide_keys,
    scores,
    probs,
    flipped,
    acc,
    top,
    total,
    k_send,
    k_recv,
    v_send,
    v_recv,
    s_send,
    s_recv,
    g_send,
    g_recv,
    f_send,
    a_send,
    a_recv,
    local_sem,
):
    me = lax.axis_index("pool")
    row = lax.axis_index("tp")
    block = pool_k.shape[1]
    head = pool_k.shape[2]
    turn = tq_ref.shape[0] // seats
    group = tq_ref.shape[1] // head
    wide = group * turn
    chips = pools // 2
    share = pools // tps
    part = weight.shape[0] // pools
    w_cols = weight.shape[1]
    sibling = me + 1 - 2 * lax.rem(me, 2)
    core = lax.rem(me, 2)
    chip = me // 2
    target_row = me // share
    at_home = target_row == row

    barrier = pltpu.get_barrier_semaphore()

    def greet(pool_index, tp_index):
        pl.semaphore_signal(barrier, inc=1, device_id=(pool_index, tp_index), device_id_type=MESH)

    def greet_pool(i, carry):
        greet(lax.rem(me + i, pools), row)
        return carry

    lax.fori_loop(1, pools, greet_pool, 0)

    @pl.when(row > 0)
    def _():
        greet(me, row - 1)

    @pl.when(row < tps - 1)
    def _():
        greet(me, row + 1)

    def greet_source(i, carry):
        source_pool = row * share + i // tps
        source_row = lax.rem(i, tps)

        @pl.when(jnp.logical_not((source_pool == me) & (source_row == row)))
        def _():
            greet(source_pool, source_row)

        return carry

    lax.fori_loop(0, share * tps, greet_source, 0)
    greeted = (
        2 * pools
        - 1
        - at_home.astype(jnp.int32)
        + (row > 0).astype(jnp.int32)
        + (row < tps - 1).astype(jnp.int32)
    )
    pl.semaphore_wait(barrier, greeted)

    def kv_copies(q):
        return (
            pltpu.make_async_remote_copy(
                src_ref=send_k.at[q],
                dst_ref=keys.at[me],
                send_sem=k_send.at[q],
                recv_sem=k_recv.at[me],
                device_id=(q, row),
                device_id_type=MESH,
            ),
            pltpu.make_async_remote_copy(
                src_ref=send_v.at[q],
                dst_ref=vals.at[me],
                send_sem=v_send.at[q],
                recv_sem=v_recv.at[me],
                device_id=(q, row),
                device_id_type=MESH,
            ),
        )

    def kv_arrival(s):
        return (
            pltpu.make_async_remote_copy(
                src_ref=keys.at[s],
                dst_ref=keys.at[s],
                send_sem=k_send.at[s],
                recv_sem=k_recv.at[s],
                device_id=(s, row),
                device_id_type=MESH,
            ),
            pltpu.make_async_remote_copy(
                src_ref=vals.at[s],
                dst_ref=vals.at[s],
                send_sem=v_send.at[s],
                recv_sem=v_recv.at[s],
                device_id=(s, row),
                device_id_type=MESH,
            ),
        )

    def scatter_copy(q):
        return pltpu.make_async_remote_copy(
            src_ref=weight.at[pl.ds(pl.multiple_of(q * part, part), part)],
            dst_ref=gathered.at[
                q,
                row,
                :,
                pl.ds(pl.multiple_of(lax.rem(me, share) * w_cols, w_cols), w_cols),
            ],
            send_sem=s_send.at[q],
            recv_sem=s_recv.at[lax.rem(me, share) * tps + row],
            device_id=(q, target_row),
            device_id_type=MESH,
        )

    own_w = pltpu.make_async_copy(
        weight.at[pl.ds(pl.multiple_of(me * part, part), part)],
        gathered.at[
            me, row, :, pl.ds(pl.multiple_of(lax.rem(me, share) * w_cols, w_cols), w_cols)
        ],
        local_sem.at[0],
    )

    def start_scatter(i, carry):
        q = lax.rem(me + i, pools)
        scatter_copy(q).start()
        return carry

    lax.fori_loop(1, pools, start_scatter, 0)

    @pl.when(at_home)
    def _():
        own_w.start()

    @pl.when(jnp.logical_not(at_home))
    def _():
        scatter_copy(me).start()

    def start_kv(i, carry):
        q = lax.rem(me + i, pools)
        for r in range(cap):
            slot = meta_ref[q, r]
            send_k[q, r] = pool_k[slot]
            send_v[q, r] = pool_v[slot]
        for copy in kv_copies(q):
            copy.start()
        return carry

    lax.fori_loop(1, pools, start_kv, 0)
    for r in range(cap):
        slot = meta_ref[me, r]
        keys[me, r] = pool_k[slot]
        vals[me, r] = pool_v[slot]

    halves = 2
    half_rows = tps // halves

    def slab_copy(slab, half, pool_index, send_sem):
        piece = gathered.at[slab, pl.ds(half * half_rows, half_rows)]
        return pltpu.make_async_remote_copy(
            src_ref=piece,
            dst_ref=piece,
            send_sem=send_sem,
            recv_sem=g_recv.at[slab, half],
            device_id=(pool_index, row),
            device_id_type=MESH,
        )

    def chip_peer(i):
        return lax.rem(chip + i, chips) * 2 + core

    def chip_source(i):
        return lax.rem(chip + chips - i, chips) * 2 + core

    relay = chips == 4
    next_x = (chip + 1 - 2 * lax.rem(chip, 2)) * 2 + core
    next_y = lax.rem(chip + 2, 4) * 2 + core
    across = (lax.rem(chip + 2, 4) + 1 - 2 * lax.rem(chip, 2)) * 2 + core

    def own_slab_sends():
        if relay:
            order = [(next_x, 0), (next_y, 1), (next_x, 1), (next_y, 0)]
            return [(me, half, peer, g_send.at[n]) for n, (peer, half) in enumerate(order)]
        return []

    def relay_sends():
        return [(next_x, 0, next_y, g_send.at[4]), (next_y, 1, next_x, g_send.at[5])]

    def core_send(n, slab, half):
        return (slab, half, sibling, f_send.at[n, half])

    def start_gather():
        def wait_piece(i, carry):
            piece_pool = row * share + i // tps
            piece_row = lax.rem(i, tps)

            @pl.when(jnp.logical_not((piece_pool == me) & (piece_row == row)))
            def _():
                landing = gathered.at[
                    me,
                    piece_row,
                    :,
                    pl.ds(pl.multiple_of((i // tps) * w_cols, w_cols), w_cols),
                ]
                pltpu.make_async_remote_copy(
                    src_ref=landing,
                    dst_ref=landing,
                    send_sem=s_send.at[0],
                    recv_sem=s_recv.at[i],
                    device_id=(piece_pool, piece_row),
                    device_id_type=MESH,
                ).wait_recv()

            return carry

        lax.fori_loop(0, share * tps, wait_piece, 0)

        @pl.when(at_home)
        def _():
            own_w.wait()

        if relay:
            for item in own_slab_sends():
                slab_copy(*item).start()
        else:

            def start_slab(i, carry):
                for half in range(halves):
                    slab_copy(me, half, chip_peer(i), g_send.at[i * halves + half]).start()
                return carry

            lax.fori_loop(1, chips, start_slab, 0)
        for half in range(halves):
            slab_copy(*core_send(0, me, half)).start()

    def pass_on(n, slab, half, onward=None):
        to_core = slab_copy(*core_send(n, slab, half))
        to_core.wait_recv()
        if onward is not None:
            slab_copy(*onward).start()
        to_core.start()

    factor = math.log2(math.e) / math.sqrt(head)
    tables = []
    for e in range(seats):
        far, near = meta_ref[4 * pools + e, 0], meta_ref[4 * pools + e, 1]
        ca, sa = cos_far[pl.ds(far, 1), :], sin_far[pl.ds(far, 1), :]
        cb, sb = cos_near[pl.ds(near, 1), :], sin_near[pl.ds(near, 1), :]
        ca, sa = ca * cb - sa * sb, sa * cb + ca * sb
        cb, sb = cos_near[...], sin_near[...]
        tables.append((ca * cb - sa * sb, sa * cb + ca * sb))

    def rope(x, cosine, sine):
        return x * cosine + pltpu.roll(x, head // 2, 1) * sine

    lanes = lax.broadcasted_iota(jnp.int32, (turn, wide), 1)
    unseen = lax.broadcasted_iota(jnp.int32, (turn, wide), 0) > lax.rem(lanes, turn)
    for e in range(seats):
        cosine, sine = tables[e]
        rows = slice(e * turn, (e + 1) * turn)
        for h in range(group):
            x = tq_ref[rows, h * head : (h + 1) * head].astype(F32)
            turned = rope(x, cosine, sine) * factor
            queries[e * head : (e + 1) * head, h * turn : (h + 1) * turn] = turned.T.astype(BF16)
        new_keys = rope(tk_ref[rows, :].astype(F32), cosine, sine).astype(BF16)
        s = jnp.where(unseen, -jnp.inf, dot(new_keys, queries[e * head : (e + 1) * head, :]))
        best = jnp.max(s, axis=0, keepdims=True)
        p = jnp.exp2(s - best)
        top[e : e + 1, :] = best
        total[e : e + 1, :] = jnp.sum(p, axis=0, keepdims=True)
        flipped_new = tv_ref[rows, :].astype(F32).T.astype(BF16)
        acc[e * head : (e + 1) * head, :] = dot(flipped_new, p.astype(BF16))

    depth = lax.broadcasted_iota(jnp.int32, (block, 1), 0)

    def attend(source):
        tops = [top[e : e + 1, :] for e in range(seats)]
        owners = []
        for b in range(cap):
            far, seat = meta_ref[pools + source, b], meta_ref[2 * pools + source, b]
            owners.append(seat)
            ca, sa = cos_far[pl.ds(far, 1), :], sin_far[pl.ds(far, 1), :]
            cb, sb = cos_near[0:block, :], sin_near[0:block, :]
            x = keys[source, b].astype(F32)
            turned = rope(x, ca * cb - sa * sb, sa * cb + ca * sb)
            upright = vals[source, b].astype(F32).T
            span = slice(b * block, (b + 1) * block)
            for e in range(seats):
                part_e = slice(e * head, (e + 1) * head)
                wide_keys[span, part_e] = jnp.where(seat == e, turned, 0.0).astype(BF16)
                flipped[part_e, span] = jnp.where(seat == e, upright, 0.0).astype(BF16)
        run = math.gcd(cap, 4)
        for first in range(0, cap, run):
            several = dot(
                wide_keys[first * block : (first + run) * block, :], queries[...]
            )
            for b in range(first, first + run):
                s = several[(b - first) * block : (b - first + 1) * block, :]
                s = jnp.where(depth < meta_ref[3 * pools + source, b], s, -jnp.inf)
                scores[b * block : (b + 1) * block, :] = s
                best = jnp.max(s, axis=0, keepdims=True)
                for e in range(seats):
                    tops[e] = jnp.maximum(tops[e], jnp.where(owners[b] == e, best, -jnp.inf))
        alphas = [jnp.exp2(top[e : e + 1, :] - tops[e]) for e in range(seats)]
        sums = [total[e : e + 1, :] * alphas[e] for e in range(seats)]
        for b in range(cap):
            span = slice(b * block, (b + 1) * block)
            base = tops[0]
            for e in range(1, seats):
                base = jnp.where(owners[b] == e, tops[e], base)
            p = jnp.exp2(scores[span, :] - base)
            added = jnp.sum(p, axis=0, keepdims=True)
            for e in range(seats):
                sums[e] = sums[e] + jnp.where(owners[b] == e, added, 0.0)
            probs[span, :] = p.astype(BF16)
        gained = dot(flipped[...], probs[...])
        for e in range(seats):
            rows = slice(e * head, (e + 1) * head)
            acc[rows, :] = acc[rows, :] * alphas[e] + gained[rows, :]
            top[e : e + 1, :] = tops[e]
            total[e : e + 1, :] = sums[e]

    def step(i, carry):
        source = lax.rem(me + pools - i, pools)

        @pl.when(i > 0)
        def _():
            for copy in kv_arrival(source):
                copy.wait_recv()

        @pl.when(i == pools - 3)
        def _():
            start_gather()

        attend(source)
        return carry

    lax.fori_loop(0, pools, step, 0)

    for e in range(seats):
        rows = slice(e * turn, (e + 1) * turn)
        final = acc[e * head : (e + 1) * head, :] / total[e : e + 1, :]
        for h in range(group):
            attended[row, rows, h * head : (h + 1) * head] = (
                final[:, h * turn : (h + 1) * turn].T.astype(BF16)
            )

    def slot_copy(slot, neighbour, way, hop):
        return pltpu.make_async_remote_copy(
            src_ref=attended.at[slot],
            dst_ref=attended.at[slot],
            send_sem=a_send.at[way, hop],
            recv_sem=a_recv.at[slot],
            device_id=(me, neighbour),
            device_id_type=MESH,
        )

    def hop_sends(hop, act):
        @pl.when((row - hop >= 0) & (row < tps - 1))
        def _():
            act(slot_copy(row - hop, row + 1, 0, hop))

        @pl.when((row + hop < tps) & (row > 0))
        def _():
            act(slot_copy(row + hop, row - 1, 1, hop))

    def hop_waits(hop):
        @pl.when(row - hop >= 0)
        def _():
            slot_copy(row - hop, row - 1, 0, 0).wait_recv()

        @pl.when(row + hop < tps)
        def _():
            slot_copy(row + hop, row + 1, 1, 0).wait_recv()

    hop_sends(0, lambda copy: copy.start())
    if relay:
        first, second = relay_sends()
        passes = [
            [(1, next_x, 0, first), (2, next_y, 1, second)],
            [(1, next_x, 1), (2, next_y, 0)],
            [(3, across, 0), (3, across, 1)],
        ]
    else:
        passes = []
    for hop in range(1, tps):
        if passes:
            for item in passes.pop(0):
                pass_on(*item)
        hop_waits(hop)
        if hop < tps - 1:
            hop_sends(hop, lambda copy: copy.start())
    for group_of in passes:
        for item in group_of:
            pass_on(*item)
    if not relay:

        def rest(i, carry):
            for half in range(halves):
                pass_on(i, chip_source(i), half)
            return carry

        lax.fori_loop(1, chips, rest, 0)

    def wait_passed(i, carry):
        slab = chip_source(i) - core + lax.rem(sibling, 2)
        for half in range(halves):
            slab_copy(slab, half, sibling, g_send.at[0]).wait_recv()
        return carry

    lax.fori_loop(0, chips, wait_passed, 0)

    tile = 256

    def project(n, carry):
        cols = pl.ds(pl.multiple_of(n * tile, tile), tile)
        result = jnp.zeros((out_ref.shape[0], tile), F32)
        for t in range(tps):
            w = gathered[:, t, :, cols].reshape(pools * part, tile)
            result = result + dot(attended[t], w)
        out_ref[:, cols] = result.astype(BF16)
        return carry

    lax.fori_loop(0, out_ref.shape[1] // tile, project, 0)

    def wait_sends(i, carry):
        q = lax.rem(me + i, pools)
        for copy in kv_copies(q):
            copy.wait_send()
        scatter_copy(q).wait_send()
        return carry

    lax.fori_loop(1, pools, wait_sends, 0)

    @pl.when(jnp.logical_not(at_home))
    def _():
        scatter_copy(me).wait_send()

    if relay:
        for item in own_slab_sends() + relay_sends():
            slab_copy(*item).wait_send()
        for n, slab in enumerate((me, next_x, next_y, across)):
            for half in range(halves):
                slab_copy(*core_send(n, slab, half)).wait_send()
    else:

        def wait_slabs(i, carry):
            for half in range(halves):
                slab_copy(me, half, chip_peer(i), g_send.at[i * halves + half]).wait_send()
                slab_copy(*core_send(i, chip_source(i), half)).wait_send()
            return carry

        lax.fori_loop(1, chips, wait_slabs, 0)
        for half in range(halves):
            slab_copy(*core_send(0, me, half)).wait_send()
    for hop in range(tps - 1):
        hop_sends(hop, lambda copy: copy.wait_send())


def plan(pools, seats, cap, blocks_here, block, seat_ref, len_ref, map_ref, out_ref):
    me = lax.axis_index("pool")
    slots, block_count = map_ref.shape[0], map_ref.shape[1]
    seated = pools * seats

    def iota(shape, dim):
        return lax.broadcasted_iota(jnp.int32, shape, dim)

    def lane_sum(mask, x):
        return jnp.sum(jnp.where(mask, x, 0.0), axis=1, keepdims=True)

    sits = seat_ref[...] == iota((seated, slots), 1)
    lengths = lane_sum(sits, len_ref[...].astype(F32))
    all_slots = map_ref[...].astype(F32)
    seat_map = jnp.zeros((seated, block_count), F32)
    for session in range(slots):
        seat_map = seat_map + jnp.where(
            seat_ref[...] == session, all_slots[session : session + 1, :], 0.0
        )
    home = jnp.floor(seat_map * (1.0 / blocks_here))
    slot = seat_map - home * blocks_here
    numbers = iota((seated, block_count), 1).astype(F32)
    alive = numbers * block < lengths
    upto = jnp.where(
        iota((block_count, block_count), 0) <= iota((block_count, block_count), 1), 1.0, 0.0
    )

    leaving = alive & (home == me.astype(F32))
    flags = jnp.where(leaving, 1.0, 0.0)
    row_a, row_b = iota((seated, seated), 0), iota((seated, seated), 1)
    before = jnp.where((row_b < row_a) & (row_b // seats == row_a // seats), 1.0, 0.0)
    offset = jnp.sum(dot(before, flags), axis=1, keepdims=True)
    rank = dot(flags, upto) - 1.0 + offset
    merge = jnp.where(
        iota((pools, seated), 0) == iota((pools, seated), 1) // seats, 1.0, 0.0
    )
    for r in range(cap):
        picked = dot(merge, jnp.where(leaving & (rank == r), slot, 0.0))
        out_ref[0:pools, r : r + 1] = jnp.sum(picked, axis=1, keepdims=True).astype(jnp.int32)

    sources = iota((pools, block_count), 0).astype(F32)
    order = iota((pools, block_count), 1).astype(F32)
    taken = jnp.zeros((pools, 1), F32)
    found = [[jnp.zeros((pools, 1), F32) for r in range(cap)] for kind in range(3)]
    rows = iota((seated, block_count), 0)
    for e in range(seats):
        mine = rows == me * seats + e
        own_home = jnp.sum(jnp.where(mine, home, 0.0), axis=0, keepdims=True)
        own_length = jnp.sum(
            jnp.where(mine, lengths + jnp.zeros_like(home), 0.0), axis=0, keepdims=True
        )
        coming = (order * block < own_length) & (own_home == sources)
        flags = jnp.where(coming, 1.0, 0.0)
        rank = dot(flags, upto) - 1.0 + taken
        taken = taken + jnp.sum(flags, axis=1, keepdims=True)
        for r in range(cap):
            hit = coming & (rank == r)
            found[0][r] = found[0][r] + lane_sum(hit, order)
            found[1][r] = found[1][r] + lane_sum(hit, jnp.full_like(order, e + 1.0))
            found[2][r] = found[2][r] + lane_sum(hit, own_length - order * block)
        length = own_length[:, 0:1]
        far = jnp.floor(length * (1.0 / block))
        out_ref[4 * pools + e : 4 * pools + e + 1, 0:1] = far.astype(jnp.int32)
        out_ref[4 * pools + e : 4 * pools + e + 1, 1:2] = (length - far * block).astype(jnp.int32)
    for kind in range(3):
        for r in range(cap):
            value = found[kind][r] - (1.0 if kind == 1 else 0.0)
            out_ref[(kind + 1) * pools : (kind + 2) * pools, r : r + 1] = value.astype(jnp.int32)


def local(
    turn_query,
    turn_key,
    turn_value,
    pool_keys,
    pool_values,
    seat_session,
    history_len,
    block_map,
    out_weight,
):
    pools = lax.axis_size("pool")
    tps = lax.axis_size("tp")
    block, head = pool_keys.shape[1:]
    block_count = block_map.shape[1]
    seats = seat_session.shape[0] // pools
    cap = seats * block_count // pools
    rows, width = turn_query.shape
    turn = rows // seats
    group = width // head
    wide = group * turn
    part = out_weight.shape[0] // pools
    out_cols = out_weight.shape[1] * pools // tps

    in_vmem = pl.BlockSpec(memory_space=pltpu.VMEM)
    in_smem = pl.BlockSpec(memory_space=pltpu.SMEM)
    anywhere = pl.BlockSpec(memory_space=pl.ANY)
    dma = pltpu.SemaphoreType.DMA

    meta = pl.pallas_call(
        functools.partial(plan, pools, seats, cap, pool_keys.shape[0], block),
        out_shape=jax.ShapeDtypeStruct((4 * pools + 8, max(cap, 2)), jnp.int32),
        in_specs=[in_vmem] * 3,
        out_specs=in_vmem,
    )(seat_session[:, None], history_len[None, :], block_map)

    half = head // 2
    inverse = rope_base ** (-2.0 * np.arange(half) / head)
    inverse = np.concatenate([inverse, inverse])
    signs = np.concatenate([-np.ones(half), np.ones(half)])
    near = np.arange(turn)[:, None] * inverse[None, :]
    far = (np.arange(block_count + 1) * block)[:, None] * inverse[None, :]
    cos_near = jnp.asarray(np.cos(near), F32)
    sin_near = jnp.asarray(np.sin(near) * signs, F32)
    cos_far = jnp.asarray(np.cos(far), F32)
    sin_far = jnp.asarray(np.sin(far) * signs, F32)

    chips = pools // 2
    return pl.pallas_call(
        functools.partial(kernel, pools, tps, seats, cap),
        out_shape=jax.ShapeDtypeStruct((rows, out_cols), BF16),
        in_specs=[in_smem] + [in_vmem] * 9 + [anywhere],
        out_specs=in_vmem,
        scratch_shapes=[
            pltpu.VMEM((pools, cap, block, head), BF16),
            pltpu.VMEM((pools, cap, block, head), BF16),
            pltpu.VMEM((pools, cap, block, head), BF16),
            pltpu.VMEM((pools, cap, block, head), BF16),
            pltpu.VMEM((pools, tps, part, out_cols), BF16),
            pltpu.VMEM((tps, rows, width), BF16),
            pltpu.VMEM((seats * head, wide), BF16),
            pltpu.VMEM((cap * block, seats * head), BF16),
            pltpu.VMEM((cap * block, wide), F32),
            pltpu.VMEM((cap * block, wide), BF16),
            pltpu.VMEM((seats * head, cap * block), BF16),
            pltpu.VMEM((seats * head, wide), F32),
            pltpu.VMEM((seats, wide), F32),
            pltpu.VMEM((seats, wide), F32),
            dma((pools,)),
            dma((pools,)),
            dma((pools,)),
            dma((pools,)),
            dma((pools,)),
            dma((pools,)),
            dma((2 * chips,)),
            dma((pools, 2)),
            dma((chips, 2)),
            dma((2, tps)),
            dma((tps,)),
            dma((1,)),
        ],
        compiler_params=pltpu.CompilerParams(
            collective_id=0, has_side_effects=True, vmem_limit_bytes=56 * 1024 * 1024
        ),
    )(
        meta,
        turn_query,
        turn_key,
        turn_value,
        cos_far,
        sin_far,
        cos_near,
        sin_near,
        pool_keys,
        pool_values,
        out_weight,
    )


def solution(mesh):
    return jax.shard_map(
        local,
        mesh=mesh,
        in_specs=(
            P("pool", "tp"),
            P("pool", "tp"),
            P("pool", "tp"),
            P("pool", None, "tp"),
            P("pool", None, "tp"),
            P(),
            P(),
            P(),
            P("tp", "pool"),
        ),
        out_specs=P("pool", "tp"),
        check_vma=False,
    )
```

```python
import functools
import math

import jax
import jax.numpy as jnp
import numpy as np
from jax import lax
from jax.experimental import pallas as pl
from jax.experimental.pallas import tpu as pltpu
from jax.sharding import PartitionSpec as P

rope_base = 1000000.0
MESH = pl.DeviceIdType.MESH
F32 = jnp.float32
BF16 = jnp.bfloat16
dot = functools.partial(jnp.dot, preferred_element_type=F32)


def kernel(
    pools,
    tps,
    seats,
    cap,
    meta_ref,
    tq_ref,
    tk_ref,
    tv_ref,
    cos_far,
    sin_far,
    cos_near,
    sin_near,
    pool_k,
    pool_v,
    weight,
    out_ref,
    send_k,
    send_v,
    keys,
    vals,
    gathered,
    attended,
    queries,
    wide_keys,
    scores,
    probs,
    flipped,
    acc,
    top,
    total,
    partial,
    k_send,
    k_recv,
    v_send,
    v_recv,
    s_send,
    s_recv,
    g_send,
    g_recv,
    f_send,
    a_send,
    a_recv,
    local_sem,
):
    me = lax.axis_index("pool")
    row = lax.axis_index("tp")
    block = pool_k.shape[1]
    head = pool_k.shape[2]
    turn = tq_ref.shape[0] // seats
    group = tq_ref.shape[1] // head
    wide = group * turn
    chips = pools // 2
    share = pools // tps
    part = weight.shape[0] // pools
    w_cols = weight.shape[1]
    sibling = me + 1 - 2 * lax.rem(me, 2)
    core = lax.rem(me, 2)
    chip = me // 2
    target_row = me // share
    at_home = target_row == row

    barrier = pltpu.get_barrier_semaphore()

    def greet(pool_index, tp_index):
        pl.semaphore_signal(barrier, inc=1, device_id=(pool_index, tp_index), device_id_type=MESH)

    def greet_pool(i, carry):
        greet(lax.rem(me + i, pools), row)
        return carry

    lax.fori_loop(1, pools, greet_pool, 0)

    @pl.when(row > 0)
    def _():
        greet(me, row - 1)

    @pl.when(row < tps - 1)
    def _():
        greet(me, row + 1)

    def greet_source(i, carry):
        source_pool = row * share + i // tps
        source_row = lax.rem(i, tps)

        @pl.when(jnp.logical_not((source_pool == me) & (source_row == row)))
        def _():
            greet(source_pool, source_row)

        return carry

    lax.fori_loop(0, share * tps, greet_source, 0)
    greeted = (
        2 * pools
        - 1
        - at_home.astype(jnp.int32)
        + (row > 0).astype(jnp.int32)
        + (row < tps - 1).astype(jnp.int32)
    )
    pl.semaphore_wait(barrier, greeted)

    def kv_copies(q):
        return (
            pltpu.make_async_remote_copy(
                src_ref=send_k.at[q],
                dst_ref=keys.at[me],
                send_sem=k_send.at[q],
                recv_sem=k_recv.at[me],
                device_id=(q, row),
                device_id_type=MESH,
            ),
            pltpu.make_async_remote_copy(
                src_ref=send_v.at[q],
                dst_ref=vals.at[me],
                send_sem=v_send.at[q],
                recv_sem=v_recv.at[me],
                device_id=(q, row),
                device_id_type=MESH,
            ),
        )

    def kv_arrival(s):
        return (
            pltpu.make_async_remote_copy(
                src_ref=keys.at[s],
                dst_ref=keys.at[s],
                send_sem=k_send.at[s],
                recv_sem=k_recv.at[s],
                device_id=(s, row),
                device_id_type=MESH,
            ),
            pltpu.make_async_remote_copy(
                src_ref=vals.at[s],
                dst_ref=vals.at[s],
                send_sem=v_send.at[s],
                recv_sem=v_recv.at[s],
                device_id=(s, row),
                device_id_type=MESH,
            ),
        )

    def scatter_copy(q):
        return pltpu.make_async_remote_copy(
            src_ref=weight.at[pl.ds(pl.multiple_of(q * part, part), part)],
            dst_ref=gathered.at[
                q,
                row,
                :,
                pl.ds(pl.multiple_of(lax.rem(me, share) * w_cols, w_cols), w_cols),
            ],
            send_sem=s_send.at[q],
            recv_sem=s_recv.at[lax.rem(me, share) * tps + row],
            device_id=(q, target_row),
            device_id_type=MESH,
        )

    own_w = pltpu.make_async_copy(
        weight.at[pl.ds(pl.multiple_of(me * part, part), part)],
        gathered.at[
            me, row, :, pl.ds(pl.multiple_of(lax.rem(me, share) * w_cols, w_cols), w_cols)
        ],
        local_sem.at[0],
    )

    def start_scatter(i, carry):
        q = lax.rem(me + i, pools)
        scatter_copy(q).start()
        return carry

    lax.fori_loop(1, pools, start_scatter, 0)

    @pl.when(at_home)
    def _():
        own_w.start()

    @pl.when(jnp.logical_not(at_home))
    def _():
        scatter_copy(me).start()

    def start_kv(i, carry):
        q = lax.rem(me + i, pools)
        for r in range(cap):
            slot = meta_ref[q, r]
            send_k[q, r] = pool_k[slot]
            send_v[q, r] = pool_v[slot]
        for copy in kv_copies(q):
            copy.start()
        return carry

    lax.fori_loop(1, pools, start_kv, 0)
    for r in range(cap):
        slot = meta_ref[me, r]
        keys[me, r] = pool_k[slot]
        vals[me, r] = pool_v[slot]

    halves = 2
    half_rows = tps // halves

    def slab_copy(slab, half, pool_index, send_sem):
        piece = gathered.at[slab, pl.ds(half * half_rows, half_rows)]
        return pltpu.make_async_remote_copy(
            src_ref=piece,
            dst_ref=piece,
            send_sem=send_sem,
            recv_sem=g_recv.at[slab, half],
            device_id=(pool_index, row),
            device_id_type=MESH,
        )

    def chip_peer(i):
        return lax.rem(chip + i, chips) * 2 + core

    def chip_source(i):
        return lax.rem(chip + chips - i, chips) * 2 + core

    relay = chips == 4
    next_x = (chip + 1 - 2 * lax.rem(chip, 2)) * 2 + core
    next_y = lax.rem(chip + 2, 4) * 2 + core
    across = (lax.rem(chip + 2, 4) + 1 - 2 * lax.rem(chip, 2)) * 2 + core

    def own_slab_sends():
        if relay:
            order = [(next_x, 0), (next_y, 1), (next_x, 1), (next_y, 0)]
            return [(me, half, peer, g_send.at[n]) for n, (peer, half) in enumerate(order)]
        return []

    def relay_sends():
        return [(next_x, 0, next_y, g_send.at[4]), (next_y, 1, next_x, g_send.at[5])]

    def core_send(n, slab, half):
        return (slab, half, sibling, f_send.at[n, half])

    def start_gather():
        def wait_piece(i, carry):
            piece_pool = row * share + i // tps
            piece_row = lax.rem(i, tps)

            @pl.when(jnp.logical_not((piece_pool == me) & (piece_row == row)))
            def _():
                landing = gathered.at[
                    me,
                    piece_row,
                    :,
                    pl.ds(pl.multiple_of((i // tps) * w_cols, w_cols), w_cols),
                ]
                pltpu.make_async_remote_copy(
                    src_ref=landing,
                    dst_ref=landing,
                    send_sem=s_send.at[0],
                    recv_sem=s_recv.at[i],
                    device_id=(piece_pool, piece_row),
                    device_id_type=MESH,
                ).wait_recv()

            return carry

        lax.fori_loop(0, share * tps, wait_piece, 0)

        @pl.when(at_home)
        def _():
            own_w.wait()

        if relay:
            for item in own_slab_sends():
                slab_copy(*item).start()
        else:

            def start_slab(i, carry):
                for half in range(halves):
                    slab_copy(me, half, chip_peer(i), g_send.at[i * halves + half]).start()
                return carry

            lax.fori_loop(1, chips, start_slab, 0)
        for half in range(halves):
            slab_copy(*core_send(0, me, half)).start()

    def pass_on(n, slab, half, onward=None):
        to_core = slab_copy(*core_send(n, slab, half))
        to_core.wait_recv()
        if onward is not None:
            slab_copy(*onward).start()
        to_core.start()

    factor = math.log2(math.e) / math.sqrt(head)
    tables = []
    for e in range(seats):
        far, near = meta_ref[4 * pools + e, 0], meta_ref[4 * pools + e, 1]
        ca, sa = cos_far[pl.ds(far, 1), :], sin_far[pl.ds(far, 1), :]
        cb, sb = cos_near[pl.ds(near, 1), :], sin_near[pl.ds(near, 1), :]
        ca, sa = ca * cb - sa * sb, sa * cb + ca * sb
        cb, sb = cos_near[...], sin_near[...]
        tables.append((ca * cb - sa * sb, sa * cb + ca * sb))

    def rope(x, cosine, sine):
        return x * cosine + pltpu.roll(x, head // 2, 1) * sine

    lanes = lax.broadcasted_iota(jnp.int32, (turn, wide), 1)
    unseen = lax.broadcasted_iota(jnp.int32, (turn, wide), 0) > lax.rem(lanes, turn)
    for e in range(seats):
        cosine, sine = tables[e]
        rows = slice(e * turn, (e + 1) * turn)
        for h in range(group):
            x = tq_ref[rows, h * head : (h + 1) * head].astype(F32)
            turned = rope(x, cosine, sine) * factor
            queries[e * head : (e + 1) * head, h * turn : (h + 1) * turn] = turned.T.astype(BF16)
        new_keys = rope(tk_ref[rows, :].astype(F32), cosine, sine).astype(BF16)
        s = jnp.where(unseen, -jnp.inf, dot(new_keys, queries[e * head : (e + 1) * head, :]))
        best = jnp.max(s, axis=0, keepdims=True)
        p = jnp.exp2(s - best)
        top[e : e + 1, :] = best
        total[e : e + 1, :] = jnp.sum(p, axis=0, keepdims=True)
        flipped_new = tv_ref[rows, :].astype(F32).T.astype(BF16)
        acc[e * head : (e + 1) * head, :] = dot(flipped_new, p.astype(BF16))

    depth = lax.broadcasted_iota(jnp.int32, (block, 1), 0)

    def attend(source):
        tops = [top[e : e + 1, :] for e in range(seats)]
        owners = []
        for b in range(cap):
            far, seat = meta_ref[pools + source, b], meta_ref[2 * pools + source, b]
            owners.append(seat)
            ca, sa = cos_far[pl.ds(far, 1), :], sin_far[pl.ds(far, 1), :]
            cb, sb = cos_near[0:block, :], sin_near[0:block, :]
            x = keys[source, b].astype(F32)
            turned = rope(x, ca * cb - sa * sb, sa * cb + ca * sb)
            upright = vals[source, b].astype(F32).T
            span = slice(b * block, (b + 1) * block)
            for e in range(seats):
                part_e = slice(e * head, (e + 1) * head)
                wide_keys[span, part_e] = jnp.where(seat == e, turned, 0.0).astype(BF16)
                flipped[part_e, span] = jnp.where(seat == e, upright, 0.0).astype(BF16)
        run = math.gcd(cap, 4)
        for first in range(0, cap, run):
            several = dot(
                wide_keys[first * block : (first + run) * block, :], queries[...]
            )
            for b in range(first, first + run):
                s = several[(b - first) * block : (b - first + 1) * block, :]
                s = jnp.where(depth < meta_ref[3 * pools + source, b], s, -jnp.inf)
                scores[b * block : (b + 1) * block, :] = s
                best = jnp.max(s, axis=0, keepdims=True)
                for e in range(seats):
                    tops[e] = jnp.maximum(tops[e], jnp.where(owners[b] == e, best, -jnp.inf))
        alphas = [jnp.exp2(top[e : e + 1, :] - tops[e]) for e in range(seats)]
        sums = [total[e : e + 1, :] * alphas[e] for e in range(seats)]
        for b in range(cap):
            span = slice(b * block, (b + 1) * block)
            base = tops[0]
            for e in range(1, seats):
                base = jnp.where(owners[b] == e, tops[e], base)
            p = jnp.exp2(scores[span, :] - base)
            added = jnp.sum(p, axis=0, keepdims=True)
            for e in range(seats):
                sums[e] = sums[e] + jnp.where(owners[b] == e, added, 0.0)
            probs[span, :] = p.astype(BF16)
        gained = dot(flipped[...], probs[...])
        for e in range(seats):
            rows = slice(e * head, (e + 1) * head)
            acc[rows, :] = acc[rows, :] * alphas[e] + gained[rows, :]
            top[e : e + 1, :] = tops[e]
            total[e : e + 1, :] = sums[e]

    def step(i, carry):
        source = lax.rem(me + pools - i, pools)

        @pl.when(i > 0)
        def _():
            for copy in kv_arrival(source):
                copy.wait_recv()

        @pl.when(i == pools - 1)
        def _():
            start_gather()

        attend(source)
        return carry

    lax.fori_loop(0, pools, step, 0)

    for e in range(seats):
        rows = slice(e * turn, (e + 1) * turn)
        final = acc[e * head : (e + 1) * head, :] / total[e : e + 1, :]
        for h in range(group):
            attended[row, rows, h * head : (h + 1) * head] = (
                final[:, h * turn : (h + 1) * turn].T.astype(BF16)
            )

    def slot_copy(slot, neighbour, way, hop):
        return pltpu.make_async_remote_copy(
            src_ref=attended.at[slot],
            dst_ref=attended.at[slot],
            send_sem=a_send.at[way, hop],
            recv_sem=a_recv.at[slot],
            device_id=(me, neighbour),
            device_id_type=MESH,
        )

    def hop_sends(hop, act):
        @pl.when((row - hop >= 0) & (row < tps - 1))
        def _():
            act(slot_copy(row - hop, row + 1, 0, hop))

        @pl.when((row + hop < tps) & (row > 0))
        def _():
            act(slot_copy(row + hop, row - 1, 1, hop))

    def hop_waits(hop):
        @pl.when(row - hop >= 0)
        def _():
            slot_copy(row - hop, row - 1, 0, 0).wait_recv()

        @pl.when(row + hop < tps)
        def _():
            slot_copy(row + hop, row + 1, 1, 0).wait_recv()

    hop_sends(0, lambda copy: copy.start())
    if relay:
        first, second = relay_sends()
        passes = [
            [(1, next_x, 0, first), (2, next_y, 1, second)],
            [(1, next_x, 1), (2, next_y, 0)],
            [(3, across, 0), (3, across, 1)],
        ]
    else:
        passes = []
    for hop in range(1, tps):
        if passes:
            for item in passes.pop(0):
                pass_on(*item)
        hop_waits(hop)
        if hop < tps - 1:
            hop_sends(hop, lambda copy: copy.start())
    for group_of in passes:
        for item in group_of:
            pass_on(*item)
    if not relay:

        def rest(i, carry):
            for half in range(halves):
                pass_on(i, chip_source(i), half)
            return carry

        lax.fori_loop(1, chips, rest, 0)

    def wait_slab(slab):
        for half in range(halves):
            slab_copy(slab, half, sibling, g_send.at[0]).wait_recv()

    tile = 512
    tiles = out_ref.shape[1] // tile
    out_rows = out_ref.shape[0]
    if relay and 2 * part == head:
        for n, slab in enumerate((me, next_x, next_y, across)):
            wait_slab(slab + sibling - me)
            pair = slab // 2
            spans = pl.ds(pl.multiple_of(pair * head, head), head)
            left = jnp.concatenate([attended[t, :, spans] for t in range(tps)], axis=1)

            def project(c, carry, n=n, pair=pair, left=left):
                cols = pl.ds(pl.multiple_of(c * tile, tile), tile)
                w = jnp.concatenate(
                    [
                        gathered[pl.ds(pair * 2, 2), t, :, cols].reshape(head, tile)
                        for t in range(tps)
                    ],
                    axis=0,
                )
                result = dot(left, w)
                if n > 0:
                    result = result + partial[:, cols]
                if n < chips - 1:
                    partial[:, cols] = result
                else:
                    out_ref[:, cols] = result.astype(BF16)
                return carry

            lax.fori_loop(0, tiles, project, 0)
    else:

        def wait_passed(i, carry):
            wait_slab(chip_source(i) + sibling - me)
            return carry

        lax.fori_loop(0, chips, wait_passed, 0)

        def project(c, carry):
            cols = pl.ds(pl.multiple_of(c * tile, tile), tile)
            result = jnp.zeros((out_rows, tile), F32)
            for t in range(tps):
                w = gathered[:, t, :, cols].reshape(pools * part, tile)
                result = result + dot(attended[t], w)
            out_ref[:, cols] = result.astype(BF16)
            return carry

        lax.fori_loop(0, tiles, project, 0)

    def wait_sends(i, carry):
        q = lax.rem(me + i, pools)
        for copy in kv_copies(q):
            copy.wait_send()
        scatter_copy(q).wait_send()
        return carry

    lax.fori_loop(1, pools, wait_sends, 0)

    @pl.when(jnp.logical_not(at_home))
    def _():
        scatter_copy(me).wait_send()

    if relay:
        for item in own_slab_sends() + relay_sends():
            slab_copy(*item).wait_send()
        for n, slab in enumerate((me, next_x, next_y, across)):
            for half in range(halves):
                slab_copy(*core_send(n, slab, half)).wait_send()
    else:

        def wait_slabs(i, carry):
            for half in range(halves):
                slab_copy(me, half, chip_peer(i), g_send.at[i * halves + half]).wait_send()
                slab_copy(*core_send(i, chip_source(i), half)).wait_send()
            return carry

        lax.fori_loop(1, chips, wait_slabs, 0)
        for half in range(halves):
            slab_copy(*core_send(0, me, half)).wait_send()
    for hop in range(tps - 1):
        hop_sends(hop, lambda copy: copy.wait_send())


def plan(pools, seats, cap, blocks_here, block, seat_ref, len_ref, map_ref, out_ref):
    me = lax.axis_index("pool")
    slots, block_count = map_ref.shape[0], map_ref.shape[1]
    seated = pools * seats

    def iota(shape, dim):
        return lax.broadcasted_iota(jnp.int32, shape, dim)

    def lane_sum(mask, x):
        return jnp.sum(jnp.where(mask, x, 0.0), axis=1, keepdims=True)

    sits = seat_ref[...] == iota((seated, slots), 1)
    lengths = lane_sum(sits, len_ref[...].astype(F32))
    all_slots = map_ref[...].astype(F32)
    seat_map = jnp.zeros((seated, block_count), F32)
    for session in range(slots):
        seat_map = seat_map + jnp.where(
            seat_ref[...] == session, all_slots[session : session + 1, :], 0.0
        )
    home = jnp.floor(seat_map * (1.0 / blocks_here))
    slot = seat_map - home * blocks_here
    numbers = iota((seated, block_count), 1).astype(F32)
    alive = numbers * block < lengths
    upto = jnp.where(
        iota((block_count, block_count), 0) <= iota((block_count, block_count), 1), 1.0, 0.0
    )

    leaving = alive & (home == me.astype(F32))
    flags = jnp.where(leaving, 1.0, 0.0)
    row_a, row_b = iota((seated, seated), 0), iota((seated, seated), 1)
    before = jnp.where((row_b < row_a) & (row_b // seats == row_a // seats), 1.0, 0.0)
    offset = jnp.sum(dot(before, flags), axis=1, keepdims=True)
    rank = dot(flags, upto) - 1.0 + offset
    merge = jnp.where(
        iota((pools, seated), 0) == iota((pools, seated), 1) // seats, 1.0, 0.0
    )
    for r in range(cap):
        picked = dot(merge, jnp.where(leaving & (rank == r), slot, 0.0))
        out_ref[0:pools, r : r + 1] = jnp.sum(picked, axis=1, keepdims=True).astype(jnp.int32)

    sources = iota((pools, block_count), 0).astype(F32)
    order = iota((pools, block_count), 1).astype(F32)
    taken = jnp.zeros((pools, 1), F32)
    found = [[jnp.zeros((pools, 1), F32) for r in range(cap)] for kind in range(3)]
    rows = iota((seated, block_count), 0)
    for e in range(seats):
        mine = rows == me * seats + e
        own_home = jnp.sum(jnp.where(mine, home, 0.0), axis=0, keepdims=True)
        own_length = jnp.sum(
            jnp.where(mine, lengths + jnp.zeros_like(home), 0.0), axis=0, keepdims=True
        )
        coming = (order * block < own_length) & (own_home == sources)
        flags = jnp.where(coming, 1.0, 0.0)
        rank = dot(flags, upto) - 1.0 + taken
        taken = taken + jnp.sum(flags, axis=1, keepdims=True)
        for r in range(cap):
            hit = coming & (rank == r)
            found[0][r] = found[0][r] + lane_sum(hit, order)
            found[1][r] = found[1][r] + lane_sum(hit, jnp.full_like(order, e + 1.0))
            found[2][r] = found[2][r] + lane_sum(hit, own_length - order * block)
        length = own_length[:, 0:1]
        far = jnp.floor(length * (1.0 / block))
        out_ref[4 * pools + e : 4 * pools + e + 1, 0:1] = far.astype(jnp.int32)
        out_ref[4 * pools + e : 4 * pools + e + 1, 1:2] = (length - far * block).astype(jnp.int32)
    for kind in range(3):
        for r in range(cap):
            value = found[kind][r] - (1.0 if kind == 1 else 0.0)
            out_ref[(kind + 1) * pools : (kind + 2) * pools, r : r + 1] = value.astype(jnp.int32)


def local(
    turn_query,
    turn_key,
    turn_value,
    pool_keys,
    pool_values,
    seat_session,
    history_len,
    block_map,
    out_weight,
):
    pools = lax.axis_size("pool")
    tps = lax.axis_size("tp")
    block, head = pool_keys.shape[1:]
    block_count = block_map.shape[1]
    seats = seat_session.shape[0] // pools
    cap = seats * block_count // pools
    rows, width = turn_query.shape
    turn = rows // seats
    group = width // head
    wide = group * turn
    part = out_weight.shape[0] // pools
    out_cols = out_weight.shape[1] * pools // tps

    in_vmem = pl.BlockSpec(memory_space=pltpu.VMEM)
    in_smem = pl.BlockSpec(memory_space=pltpu.SMEM)
    anywhere = pl.BlockSpec(memory_space=pl.ANY)
    dma = pltpu.SemaphoreType.DMA

    meta = pl.pallas_call(
        functools.partial(plan, pools, seats, cap, pool_keys.shape[0], block),
        out_shape=jax.ShapeDtypeStruct((4 * pools + 8, max(cap, 2)), jnp.int32),
        in_specs=[in_vmem] * 3,
        out_specs=in_vmem,
    )(seat_session[:, None], history_len[None, :], block_map)

    half = head // 2
    inverse = rope_base ** (-2.0 * np.arange(half) / head)
    inverse = np.concatenate([inverse, inverse])
    signs = np.concatenate([-np.ones(half), np.ones(half)])
    near = np.arange(turn)[:, None] * inverse[None, :]
    far = (np.arange(block_count + 1) * block)[:, None] * inverse[None, :]
    cos_near = jnp.asarray(np.cos(near), F32)
    sin_near = jnp.asarray(np.sin(near) * signs, F32)
    cos_far = jnp.asarray(np.cos(far), F32)
    sin_far = jnp.asarray(np.sin(far) * signs, F32)

    chips = pools // 2
    return pl.pallas_call(
        functools.partial(kernel, pools, tps, seats, cap),
        out_shape=jax.ShapeDtypeStruct((rows, out_cols), BF16),
        in_specs=[in_smem] + [in_vmem] * 9 + [anywhere],
        out_specs=in_vmem,
        scratch_shapes=[
            pltpu.VMEM((pools, cap, block, head), BF16),
            pltpu.VMEM((pools, cap, block, head), BF16),
            pltpu.VMEM((pools, cap, block, head), BF16),
            pltpu.VMEM((pools, cap, block, head), BF16),
            pltpu.VMEM((pools, tps, part, out_cols), BF16),
            pltpu.VMEM((tps, rows, width), BF16),
            pltpu.VMEM((seats * head, wide), BF16),
            pltpu.VMEM((cap * block, seats * head), BF16),
            pltpu.VMEM((cap * block, wide), F32),
            pltpu.VMEM((cap * block, wide), BF16),
            pltpu.VMEM((seats * head, cap * block), BF16),
            pltpu.VMEM((seats * head, wide), F32),
            pltpu.VMEM((seats, wide), F32),
            pltpu.VMEM((seats, wide), F32),
            pltpu.VMEM((rows, out_cols), F32),
            dma((pools,)),
            dma((pools,)),
            dma((pools,)),
            dma((pools,)),
            dma((pools,)),
            dma((pools,)),
            dma((2 * chips,)),
            dma((pools, 2)),
            dma((chips, 2)),
            dma((2, tps)),
            dma((tps,)),
            dma((1,)),
        ],
        compiler_params=pltpu.CompilerParams(
            collective_id=0, has_side_effects=True, vmem_limit_bytes=56 * 1024 * 1024
        ),
    )(
        meta,
        turn_query,
        turn_key,
        turn_value,
        cos_far,
        sin_far,
        cos_near,
        sin_near,
        pool_keys,
        pool_values,
        out_weight,
    )


def solution(mesh):
    return jax.shard_map(
        local,
        mesh=mesh,
        in_specs=(
            P("pool", "tp"),
            P("pool", "tp"),
            P("pool", "tp"),
            P("pool", None, "tp"),
            P("pool", None, "tp"),
            P(),
            P(),
            P(),
            P("tp", "pool"),
        ),
        out_specs=P("pool", "tp"),
        check_vma=False,
    )
```

```python
import functools
import math

import jax
import jax.numpy as jnp
import numpy as np
from jax import lax
from jax.experimental import pallas as pl
from jax.experimental.pallas import tpu as pltpu
from jax.sharding import PartitionSpec as P

rope_base = 1000000.0
MESH = pl.DeviceIdType.MESH
F32 = jnp.float32
BF16 = jnp.bfloat16
dot = functools.partial(jnp.dot, preferred_element_type=F32)


def kernel(
    pools,
    tps,
    seats,
    cap,
    meta_ref,
    tq_ref,
    tk_ref,
    tv_ref,
    cos_far,
    sin_far,
    cos_near,
    sin_near,
    pool_k,
    pool_v,
    weight,
    out_ref,
    send_k,
    send_v,
    keys,
    vals,
    gathered,
    attended,
    queries,
    wide_keys,
    scores,
    probs,
    flipped,
    acc,
    top,
    total,
    partial,
    k_send,
    k_recv,
    v_send,
    v_recv,
    s_send,
    s_recv,
    g_send,
    g_recv,
    f_send,
    a_send,
    a_recv,
    local_sem,
):
    me = lax.axis_index("pool")
    row = lax.axis_index("tp")
    block = pool_k.shape[1]
    head = pool_k.shape[2]
    turn = tq_ref.shape[0] // seats
    group = tq_ref.shape[1] // head
    wide = group * turn
    chips = pools // 2
    share = pools // tps
    part = weight.shape[0] // pools
    w_cols = weight.shape[1]
    sibling = me + 1 - 2 * lax.rem(me, 2)
    core = lax.rem(me, 2)
    chip = me // 2
    target_row = me // share
    at_home = target_row == row

    barrier = pltpu.get_barrier_semaphore()

    def greet(pool_index, tp_index):
        pl.semaphore_signal(barrier, inc=1, device_id=(pool_index, tp_index), device_id_type=MESH)

    def greet_pool(i, carry):
        greet(lax.rem(me + i, pools), row)
        return carry

    lax.fori_loop(1, pools, greet_pool, 0)

    @pl.when(row > 0)
    def _():
        greet(me, row - 1)

    @pl.when(row < tps - 1)
    def _():
        greet(me, row + 1)

    def greet_source(i, carry):
        source_pool = row * share + i // tps
        source_row = lax.rem(i, tps)

        @pl.when(jnp.logical_not((source_pool == me) & (source_row == row)))
        def _():
            greet(source_pool, source_row)

        return carry

    lax.fori_loop(0, share * tps, greet_source, 0)
    greeted = (
        2 * pools
        - 1
        - at_home.astype(jnp.int32)
        + (row > 0).astype(jnp.int32)
        + (row < tps - 1).astype(jnp.int32)
    )
    pl.semaphore_wait(barrier, greeted)

    def kv_copies(q):
        return (
            pltpu.make_async_remote_copy(
                src_ref=send_k.at[q],
                dst_ref=keys.at[me],
                send_sem=k_send.at[q],
                recv_sem=k_recv.at[me],
                device_id=(q, row),
                device_id_type=MESH,
            ),
            pltpu.make_async_remote_copy(
                src_ref=send_v.at[q],
                dst_ref=vals.at[me],
                send_sem=v_send.at[q],
                recv_sem=v_recv.at[me],
                device_id=(q, row),
                device_id_type=MESH,
            ),
        )

    def kv_arrival(s):
        return (
            pltpu.make_async_remote_copy(
                src_ref=keys.at[s],
                dst_ref=keys.at[s],
                send_sem=k_send.at[s],
                recv_sem=k_recv.at[s],
                device_id=(s, row),
                device_id_type=MESH,
            ),
            pltpu.make_async_remote_copy(
                src_ref=vals.at[s],
                dst_ref=vals.at[s],
                send_sem=v_send.at[s],
                recv_sem=v_recv.at[s],
                device_id=(s, row),
                device_id_type=MESH,
            ),
        )

    def scatter_copy(q):
        return pltpu.make_async_remote_copy(
            src_ref=weight.at[pl.ds(pl.multiple_of(q * part, part), part)],
            dst_ref=gathered.at[
                q,
                row,
                :,
                pl.ds(pl.multiple_of(lax.rem(me, share) * w_cols, w_cols), w_cols),
            ],
            send_sem=s_send.at[q],
            recv_sem=s_recv.at[lax.rem(me, share) * tps + row],
            device_id=(q, target_row),
            device_id_type=MESH,
        )

    own_w = pltpu.make_async_copy(
        weight.at[pl.ds(pl.multiple_of(me * part, part), part)],
        gathered.at[
            me, row, :, pl.ds(pl.multiple_of(lax.rem(me, share) * w_cols, w_cols), w_cols)
        ],
        local_sem.at[0],
    )

    def start_scatter(i, carry):
        q = lax.rem(me + i, pools)
        scatter_copy(q).start()
        return carry

    lax.fori_loop(1, pools, start_scatter, 0)

    @pl.when(at_home)
    def _():
        own_w.start()

    @pl.when(jnp.logical_not(at_home))
    def _():
        scatter_copy(me).start()

    def send_to(i):
        if chips != 4:
            return lax.rem(me + i, pools)
        x = lax.rem(lax.rem(chip, 2) + lax.rem(i, 2), 2)
        y = lax.rem(chip // 2 + lax.rem(i, 4) // 2, 2)
        return (y * 2 + x) * 2 + lax.rem(core + i // 4, 2)

    def sent_from(i):
        if chips != 4:
            return lax.rem(me + pools - i, pools)
        return send_to(i)

    def start_kv(i, carry):
        q = send_to(i)
        for r in range(cap):
            slot = meta_ref[q, r]
            send_k[q, r] = pool_k[slot]
            send_v[q, r] = pool_v[slot]
        for copy in kv_copies(q):
            copy.start()
        return carry

    in_flight = min(3, pools - 1)
    lax.fori_loop(1, 1 + in_flight, start_kv, 0)
    for r in range(cap):
        slot = meta_ref[me, r]
        keys[me, r] = pool_k[slot]
        vals[me, r] = pool_v[slot]

    halves = 2
    half_rows = tps // halves

    def slab_copy(slab, half, pool_index, send_sem):
        piece = gathered.at[slab, pl.ds(half * half_rows, half_rows)]
        return pltpu.make_async_remote_copy(
            src_ref=piece,
            dst_ref=piece,
            send_sem=send_sem,
            recv_sem=g_recv.at[slab, half],
            device_id=(pool_index, row),
            device_id_type=MESH,
        )

    def chip_peer(i):
        return lax.rem(chip + i, chips) * 2 + core

    def chip_source(i):
        return lax.rem(chip + chips - i, chips) * 2 + core

    relay = chips == 4
    next_x = (chip + 1 - 2 * lax.rem(chip, 2)) * 2 + core
    next_y = lax.rem(chip + 2, 4) * 2 + core
    across = (lax.rem(chip + 2, 4) + 1 - 2 * lax.rem(chip, 2)) * 2 + core

    def own_slab_sends():
        if relay:
            order = [(next_x, 0), (next_y, 1), (next_x, 1), (next_y, 0)]
            return [(me, half, peer, g_send.at[n]) for n, (peer, half) in enumerate(order)]
        return []

    def relay_sends():
        return [(next_x, 0, next_y, g_send.at[4]), (next_y, 1, next_x, g_send.at[5])]

    def core_send(n, slab, half):
        return (slab, half, sibling, f_send.at[n, half])

    def start_gather():
        def wait_piece(i, carry):
            piece_pool = row * share + i // tps
            piece_row = lax.rem(i, tps)

            @pl.when(jnp.logical_not((piece_pool == me) & (piece_row == row)))
            def _():
                landing = gathered.at[
                    me,
                    piece_row,
                    :,
                    pl.ds(pl.multiple_of((i // tps) * w_cols, w_cols), w_cols),
                ]
                pltpu.make_async_remote_copy(
                    src_ref=landing,
                    dst_ref=landing,
                    send_sem=s_send.at[0],
                    recv_sem=s_recv.at[i],
                    device_id=(piece_pool, piece_row),
                    device_id_type=MESH,
                ).wait_recv()

            return carry

        lax.fori_loop(0, share * tps, wait_piece, 0)

        @pl.when(at_home)
        def _():
            own_w.wait()

        if relay:
            for item in own_slab_sends():
                slab_copy(*item).start()
        else:

            def start_slab(i, carry):
                for half in range(halves):
                    slab_copy(me, half, chip_peer(i), g_send.at[i * halves + half]).start()
                return carry

            lax.fori_loop(1, chips, start_slab, 0)
        for half in range(halves):
            slab_copy(*core_send(0, me, half)).start()

    def pass_on(n, slab, half, onward=None):
        to_core = slab_copy(*core_send(n, slab, half))
        to_core.wait_recv()
        if onward is not None:
            slab_copy(*onward).start()
        to_core.start()

    factor = math.log2(math.e) / math.sqrt(head)
    tables = []
    for e in range(seats):
        far, near = meta_ref[4 * pools + e, 0], meta_ref[4 * pools + e, 1]
        ca, sa = cos_far[pl.ds(far, 1), :], sin_far[pl.ds(far, 1), :]
        cb, sb = cos_near[pl.ds(near, 1), :], sin_near[pl.ds(near, 1), :]
        ca, sa = ca * cb - sa * sb, sa * cb + ca * sb
        cb, sb = cos_near[...], sin_near[...]
        tables.append((ca * cb - sa * sb, sa * cb + ca * sb))

    def rope(x, cosine, sine):
        return x * cosine + pltpu.roll(x, head // 2, 1) * sine

    lanes = lax.broadcasted_iota(jnp.int32, (turn, wide), 1)
    unseen = lax.broadcasted_iota(jnp.int32, (turn, wide), 0) > lax.rem(lanes, turn)
    for e in range(seats):
        cosine, sine = tables[e]
        rows = slice(e * turn, (e + 1) * turn)
        for h in range(group):
            x = tq_ref[rows, h * head : (h + 1) * head].astype(F32)
            turned = rope(x, cosine, sine) * factor
            queries[e * head : (e + 1) * head, h * turn : (h + 1) * turn] = turned.T.astype(BF16)
        new_keys = rope(tk_ref[rows, :].astype(F32), cosine, sine).astype(BF16)
        s = jnp.where(unseen, -jnp.inf, dot(new_keys, queries[e * head : (e + 1) * head, :]))
        best = jnp.max(s, axis=0, keepdims=True)
        p = jnp.exp2(s - best)
        top[e : e + 1, :] = best
        total[e : e + 1, :] = jnp.sum(p, axis=0, keepdims=True)
        flipped_new = tv_ref[rows, :].astype(F32).T.astype(BF16)
        acc[e * head : (e + 1) * head, :] = dot(flipped_new, p.astype(BF16))

    depth = lax.broadcasted_iota(jnp.int32, (block, 1), 0)

    def attend(source):
        tops = [top[e : e + 1, :] for e in range(seats)]
        owners = []
        for b in range(cap):
            far, seat = meta_ref[pools + source, b], meta_ref[2 * pools + source, b]
            owners.append(seat)
            ca, sa = cos_far[pl.ds(far, 1), :], sin_far[pl.ds(far, 1), :]
            cb, sb = cos_near[0:block, :], sin_near[0:block, :]
            x = keys[source, b].astype(F32)
            turned = rope(x, ca * cb - sa * sb, sa * cb + ca * sb)
            upright = vals[source, b].astype(F32).T
            span = slice(b * block, (b + 1) * block)
            for e in range(seats):
                part_e = slice(e * head, (e + 1) * head)
                wide_keys[span, part_e] = jnp.where(seat == e, turned, 0.0).astype(BF16)
                flipped[part_e, span] = jnp.where(seat == e, upright, 0.0).astype(BF16)
        run = math.gcd(cap, 4)
        for first in range(0, cap, run):
            several = dot(
                wide_keys[first * block : (first + run) * block, :], queries[...]
            )
            for b in range(first, first + run):
                s = several[(b - first) * block : (b - first + 1) * block, :]
                s = jnp.where(depth < meta_ref[3 * pools + source, b], s, -jnp.inf)
                scores[b * block : (b + 1) * block, :] = s
                best = jnp.max(s, axis=0, keepdims=True)
                for e in range(seats):
                    tops[e] = jnp.maximum(tops[e], jnp.where(owners[b] == e, best, -jnp.inf))
        alphas = [jnp.exp2(top[e : e + 1, :] - tops[e]) for e in range(seats)]
        sums = [total[e : e + 1, :] * alphas[e] for e in range(seats)]
        for b in range(cap):
            span = slice(b * block, (b + 1) * block)
            base = tops[0]
            for e in range(1, seats):
                base = jnp.where(owners[b] == e, tops[e], base)
            p = jnp.exp2(scores[span, :] - base)
            added = jnp.sum(p, axis=0, keepdims=True)
            for e in range(seats):
                sums[e] = sums[e] + jnp.where(owners[b] == e, added, 0.0)
            probs[span, :] = p.astype(BF16)
        gained = dot(flipped[...], probs[...])
        for e in range(seats):
            rows = slice(e * head, (e + 1) * head)
            acc[rows, :] = acc[rows, :] * alphas[e] + gained[rows, :]
            top[e : e + 1, :] = tops[e]
            total[e : e + 1, :] = sums[e]

    def step(i, carry):
        source = sent_from(i)

        @pl.when(i > 0)
        def _():
            for copy in kv_arrival(source):
                copy.wait_recv()
            for copy in kv_copies(send_to(i)):
                copy.wait_send()

        @pl.when((i > 0) & (i < pools - in_flight))
        def _():
            start_kv(i + in_flight, 0)

        @pl.when(i == pools - 2)
        def _():
            start_gather()

        attend(source)
        return carry

    lax.fori_loop(0, pools, step, 0)

    for e in range(seats):
        rows = slice(e * turn, (e + 1) * turn)
        final = acc[e * head : (e + 1) * head, :] / total[e : e + 1, :]
        for h in range(group):
            attended[row, rows, h * head : (h + 1) * head] = (
                final[:, h * turn : (h + 1) * turn].T.astype(BF16)
            )

    def slot_copy(slot, neighbour, way, hop):
        return pltpu.make_async_remote_copy(
            src_ref=attended.at[slot],
            dst_ref=attended.at[slot],
            send_sem=a_send.at[way, hop],
            recv_sem=a_recv.at[slot],
            device_id=(me, neighbour),
            device_id_type=MESH,
        )

    def hop_sends(hop, act):
        @pl.when((row - hop >= 0) & (row < tps - 1))
        def _():
            act(slot_copy(row - hop, row + 1, 0, hop))

        @pl.when((row + hop < tps) & (row > 0))
        def _():
            act(slot_copy(row + hop, row - 1, 1, hop))

    def hop_waits(hop):
        @pl.when(row - hop >= 0)
        def _():
            slot_copy(row - hop, row - 1, 0, 0).wait_recv()

        @pl.when(row + hop < tps)
        def _():
            slot_copy(row + hop, row + 1, 1, 0).wait_recv()

    hop_sends(0, lambda copy: copy.start())
    if relay:
        first, second = relay_sends()
        passes = [
            [(1, next_x, 0, first), (2, next_y, 1, second)],
            [(1, next_x, 1), (2, next_y, 0)],
            [(3, across, 0), (3, across, 1)],
        ]
    else:
        passes = []
    for hop in range(1, tps):
        if passes:
            for item in passes.pop(0):
                pass_on(*item)
        hop_waits(hop)
        if hop < tps - 1:
            hop_sends(hop, lambda copy: copy.start())
    for group_of in passes:
        for item in group_of:
            pass_on(*item)
    if not relay:

        def rest(i, carry):
            for half in range(halves):
                pass_on(i, chip_source(i), half)
            return carry

        lax.fori_loop(1, chips, rest, 0)

    def wait_slab(slab):
        for half in range(halves):
            slab_copy(slab, half, sibling, g_send.at[0]).wait_recv()

    tile = 512
    tiles = out_ref.shape[1] // tile
    out_rows = out_ref.shape[0]
    if relay and 2 * part == head:
        for n, slab in enumerate((me, next_x, next_y, across)):
            wait_slab(slab + sibling - me)
            pair = slab // 2
            spans = pl.ds(pl.multiple_of(pair * head, head), head)
            left = jnp.concatenate([attended[t, :, spans] for t in range(tps)], axis=1)

            def project(c, carry, n=n, pair=pair, left=left):
                cols = pl.ds(pl.multiple_of(c * tile, tile), tile)
                w = jnp.concatenate(
                    [
                        gathered[pl.ds(pair * 2, 2), t, :, cols].reshape(head, tile)
                        for t in range(tps)
                    ],
                    axis=0,
                )
                result = dot(left, w)
                if n > 0:
                    result = result + partial[:, cols]
                if n < chips - 1:
                    partial[:, cols] = result
                else:
                    out_ref[:, cols] = result.astype(BF16)
                return carry

            lax.fori_loop(0, tiles, project, 0)
    else:

        def wait_passed(i, carry):
            wait_slab(chip_source(i) + sibling - me)
            return carry

        lax.fori_loop(0, chips, wait_passed, 0)

        def project(c, carry):
            cols = pl.ds(pl.multiple_of(c * tile, tile), tile)
            result = jnp.zeros((out_rows, tile), F32)
            for t in range(tps):
                w = gathered[:, t, :, cols].reshape(pools * part, tile)
                result = result + dot(attended[t], w)
            out_ref[:, cols] = result.astype(BF16)
            return carry

        lax.fori_loop(0, tiles, project, 0)

    def wait_sends(i, carry):
        q = lax.rem(me + i, pools)
        scatter_copy(q).wait_send()
        return carry

    lax.fori_loop(1, pools, wait_sends, 0)

    @pl.when(jnp.logical_not(at_home))
    def _():
        scatter_copy(me).wait_send()

    if relay:
        for item in own_slab_sends() + relay_sends():
            slab_copy(*item).wait_send()
        for n, slab in enumerate((me, next_x, next_y, across)):
            for half in range(halves):
                slab_copy(*core_send(n, slab, half)).wait_send()
    else:

        def wait_slabs(i, carry):
            for half in range(halves):
                slab_copy(me, half, chip_peer(i), g_send.at[i * halves + half]).wait_send()
                slab_copy(*core_send(i, chip_source(i), half)).wait_send()
            return carry

        lax.fori_loop(1, chips, wait_slabs, 0)
        for half in range(halves):
            slab_copy(*core_send(0, me, half)).wait_send()
    for hop in range(tps - 1):
        hop_sends(hop, lambda copy: copy.wait_send())


def plan(pools, seats, cap, blocks_here, block, seat_ref, len_ref, map_ref, out_ref):
    me = lax.axis_index("pool")
    slots, block_count = map_ref.shape[0], map_ref.shape[1]
    seated = pools * seats

    def iota(shape, dim):
        return lax.broadcasted_iota(jnp.int32, shape, dim)

    def lane_sum(mask, x):
        return jnp.sum(jnp.where(mask, x, 0.0), axis=1, keepdims=True)

    sits = seat_ref[...] == iota((seated, slots), 1)
    lengths = lane_sum(sits, len_ref[...].astype(F32))
    all_slots = map_ref[...].astype(F32)
    seat_map = jnp.zeros((seated, block_count), F32)
    for session in range(slots):
        seat_map = seat_map + jnp.where(
            seat_ref[...] == session, all_slots[session : session + 1, :], 0.0
        )
    home = jnp.floor(seat_map * (1.0 / blocks_here))
    slot = seat_map - home * blocks_here
    numbers = iota((seated, block_count), 1).astype(F32)
    alive = numbers * block < lengths
    upto = jnp.where(
        iota((block_count, block_count), 0) <= iota((block_count, block_count), 1), 1.0, 0.0
    )

    leaving = alive & (home == me.astype(F32))
    flags = jnp.where(leaving, 1.0, 0.0)
    row_a, row_b = iota((seated, seated), 0), iota((seated, seated), 1)
    before = jnp.where((row_b < row_a) & (row_b // seats == row_a // seats), 1.0, 0.0)
    offset = jnp.sum(dot(before, flags), axis=1, keepdims=True)
    rank = dot(flags, upto) - 1.0 + offset
    merge = jnp.where(
        iota((pools, seated), 0) == iota((pools, seated), 1) // seats, 1.0, 0.0
    )
    for r in range(cap):
        picked = dot(merge, jnp.where(leaving & (rank == r), slot, 0.0))
        out_ref[0:pools, r : r + 1] = jnp.sum(picked, axis=1, keepdims=True).astype(jnp.int32)

    sources = iota((pools, block_count), 0).astype(F32)
    order = iota((pools, block_count), 1).astype(F32)
    taken = jnp.zeros((pools, 1), F32)
    found = [[jnp.zeros((pools, 1), F32) for r in range(cap)] for kind in range(3)]
    rows = iota((seated, block_count), 0)
    for e in range(seats):
        mine = rows == me * seats + e
        own_home = jnp.sum(jnp.where(mine, home, 0.0), axis=0, keepdims=True)
        own_length = jnp.sum(
            jnp.where(mine, lengths + jnp.zeros_like(home), 0.0), axis=0, keepdims=True
        )
        coming = (order * block < own_length) & (own_home == sources)
        flags = jnp.where(coming, 1.0, 0.0)
        rank = dot(flags, upto) - 1.0 + taken
        taken = taken + jnp.sum(flags, axis=1, keepdims=True)
        for r in range(cap):
            hit = coming & (rank == r)
            found[0][r] = found[0][r] + lane_sum(hit, order)
            found[1][r] = found[1][r] + lane_sum(hit, jnp.full_like(order, e + 1.0))
            found[2][r] = found[2][r] + lane_sum(hit, own_length - order * block)
        length = own_length[:, 0:1]
        far = jnp.floor(length * (1.0 / block))
        out_ref[4 * pools + e : 4 * pools + e + 1, 0:1] = far.astype(jnp.int32)
        out_ref[4 * pools + e : 4 * pools + e + 1, 1:2] = (length - far * block).astype(jnp.int32)
    for kind in range(3):
        for r in range(cap):
            value = found[kind][r] - (1.0 if kind == 1 else 0.0)
            out_ref[(kind + 1) * pools : (kind + 2) * pools, r : r + 1] = value.astype(jnp.int32)


def local(
    turn_query,
    turn_key,
    turn_value,
    pool_keys,
    pool_values,
    seat_session,
    history_len,
    block_map,
    out_weight,
):
    pools = lax.axis_size("pool")
    tps = lax.axis_size("tp")
    block, head = pool_keys.shape[1:]
    block_count = block_map.shape[1]
    seats = seat_session.shape[0] // pools
    cap = seats * block_count // pools
    rows, width = turn_query.shape
    turn = rows // seats
    group = width // head
    wide = group * turn
    part = out_weight.shape[0] // pools
    out_cols = out_weight.shape[1] * pools // tps

    in_vmem = pl.BlockSpec(memory_space=pltpu.VMEM)
    in_smem = pl.BlockSpec(memory_space=pltpu.SMEM)
    anywhere = pl.BlockSpec(memory_space=pl.ANY)
    dma = pltpu.SemaphoreType.DMA

    meta = pl.pallas_call(
        functools.partial(plan, pools, seats, cap, pool_keys.shape[0], block),
        out_shape=jax.ShapeDtypeStruct((4 * pools + 8, max(cap, 2)), jnp.int32),
        in_specs=[in_vmem] * 3,
        out_specs=in_vmem,
    )(seat_session[:, None], history_len[None, :], block_map)

    half = head // 2
    inverse = rope_base ** (-2.0 * np.arange(half) / head)
    inverse = np.concatenate([inverse, inverse])
    signs = np.concatenate([-np.ones(half), np.ones(half)])
    near = np.arange(turn)[:, None] * inverse[None, :]
    far = (np.arange(block_count + 1) * block)[:, None] * inverse[None, :]
    cos_near = jnp.asarray(np.cos(near), F32)
    sin_near = jnp.asarray(np.sin(near) * signs, F32)
    cos_far = jnp.asarray(np.cos(far), F32)
    sin_far = jnp.asarray(np.sin(far) * signs, F32)

    chips = pools // 2
    return pl.pallas_call(
        functools.partial(kernel, pools, tps, seats, cap),
        out_shape=jax.ShapeDtypeStruct((rows, out_cols), BF16),
        in_specs=[in_smem] + [in_vmem] * 9 + [anywhere],
        out_specs=in_vmem,
        scratch_shapes=[
            pltpu.VMEM((pools, cap, block, head), BF16),
            pltpu.VMEM((pools, cap, block, head), BF16),
            pltpu.VMEM((pools, cap, block, head), BF16),
            pltpu.VMEM((pools, cap, block, head), BF16),
            pltpu.VMEM((pools, tps, part, out_cols), BF16),
            pltpu.VMEM((tps, rows, width), BF16),
            pltpu.VMEM((seats * head, wide), BF16),
            pltpu.VMEM((cap * block, seats * head), BF16),
            pltpu.VMEM((cap * block, wide), F32),
            pltpu.VMEM((cap * block, wide), BF16),
            pltpu.VMEM((seats * head, cap * block), BF16),
            pltpu.VMEM((seats * head, wide), F32),
            pltpu.VMEM((seats, wide), F32),
            pltpu.VMEM((seats, wide), F32),
            pltpu.VMEM((rows, out_cols), F32),
            dma((pools,)),
            dma((pools,)),
            dma((pools,)),
            dma((pools,)),
            dma((pools,)),
            dma((pools,)),
            dma((2 * chips,)),
            dma((pools, 2)),
            dma((chips, 2)),
            dma((2, tps)),
            dma((tps,)),
            dma((1,)),
        ],
        compiler_params=pltpu.CompilerParams(
            collective_id=0, has_side_effects=True, vmem_limit_bytes=56 * 1024 * 1024
        ),
    )(
        meta,
        turn_query,
        turn_key,
        turn_value,
        cos_far,
        sin_far,
        cos_near,
        sin_near,
        pool_keys,
        pool_values,
        out_weight,
    )


def solution(mesh):
    return jax.shard_map(
        local,
        mesh=mesh,
        in_specs=(
            P("pool", "tp"),
            P("pool", "tp"),
            P("pool", "tp"),
            P("pool", None, "tp"),
            P("pool", None, "tp"),
            P(),
            P(),
            P(),
            P("tp", "pool"),
        ),
        out_specs=P("pool", "tp"),
        check_vma=False,
    )
```

```python
import functools
import math

import jax
import jax.numpy as jnp
import numpy as np
from jax import lax
from jax.experimental import pallas as pl
from jax.experimental.pallas import tpu as pltpu
from jax.sharding import PartitionSpec as P

rope_base = 1000000.0
MESH = pl.DeviceIdType.MESH
F32 = jnp.float32
BF16 = jnp.bfloat16
dot = functools.partial(jnp.dot, preferred_element_type=F32)


def kernel(
    pools,
    tps,
    seats,
    cap,
    meta_ref,
    tq_ref,
    tk_ref,
    tv_ref,
    cos_far,
    sin_far,
    cos_near,
    sin_near,
    pool_k,
    pool_v,
    weight,
    out_ref,
    send_k,
    send_v,
    keys,
    vals,
    gathered,
    attended,
    queries,
    wide_keys,
    scores,
    probs,
    flipped,
    acc,
    top,
    total,
    partial,
    k_send,
    k_recv,
    v_send,
    v_recv,
    s_send,
    s_recv,
    g_send,
    g_recv,
    f_send,
    a_send,
    a_recv,
    local_sem,
):
    me = lax.axis_index("pool")
    row = lax.axis_index("tp")
    block = pool_k.shape[1]
    head = pool_k.shape[2]
    turn = tq_ref.shape[0] // seats
    group = tq_ref.shape[1] // head
    wide = group * turn
    chips = pools // 2
    share = pools // tps
    part = weight.shape[0] // pools
    w_cols = weight.shape[1]
    sibling = me + 1 - 2 * lax.rem(me, 2)
    core = lax.rem(me, 2)
    chip = me // 2
    target_row = me // share
    at_home = target_row == row

    barrier = pltpu.get_barrier_semaphore()

    def greet(pool_index, tp_index):
        pl.semaphore_signal(barrier, inc=1, device_id=(pool_index, tp_index), device_id_type=MESH)

    def greet_pool(i, carry):
        greet(lax.rem(me + i, pools), row)
        return carry

    lax.fori_loop(1, pools, greet_pool, 0)

    @pl.when(row > 0)
    def _():
        greet(me, row - 1)

    @pl.when(row < tps - 1)
    def _():
        greet(me, row + 1)

    def greet_source(i, carry):
        source_pool = row * share + i // tps
        source_row = lax.rem(i, tps)

        @pl.when(jnp.logical_not((source_pool == me) & (source_row == row)))
        def _():
            greet(source_pool, source_row)

        return carry

    lax.fori_loop(0, share * tps, greet_source, 0)
    greeted = (
        2 * pools
        - 1
        - at_home.astype(jnp.int32)
        + (row > 0).astype(jnp.int32)
        + (row < tps - 1).astype(jnp.int32)
    )
    pl.semaphore_wait(barrier, greeted)

    def kv_copies(q):
        return (
            pltpu.make_async_remote_copy(
                src_ref=send_k.at[q],
                dst_ref=keys.at[me],
                send_sem=k_send.at[q],
                recv_sem=k_recv.at[me],
                device_id=(q, row),
                device_id_type=MESH,
            ),
            pltpu.make_async_remote_copy(
                src_ref=send_v.at[q],
                dst_ref=vals.at[me],
                send_sem=v_send.at[q],
                recv_sem=v_recv.at[me],
                device_id=(q, row),
                device_id_type=MESH,
            ),
        )

    def kv_arrival(s):
        return (
            pltpu.make_async_remote_copy(
                src_ref=keys.at[s],
                dst_ref=keys.at[s],
                send_sem=k_send.at[s],
                recv_sem=k_recv.at[s],
                device_id=(s, row),
                device_id_type=MESH,
            ),
            pltpu.make_async_remote_copy(
                src_ref=vals.at[s],
                dst_ref=vals.at[s],
                send_sem=v_send.at[s],
                recv_sem=v_recv.at[s],
                device_id=(s, row),
                device_id_type=MESH,
            ),
        )

    def scatter_copy(q):
        return pltpu.make_async_remote_copy(
            src_ref=weight.at[pl.ds(pl.multiple_of(q * part, part), part)],
            dst_ref=gathered.at[
                q,
                row,
                :,
                pl.ds(pl.multiple_of(lax.rem(me, share) * w_cols, w_cols), w_cols),
            ],
            send_sem=s_send.at[q],
            recv_sem=s_recv.at[lax.rem(me, share) * tps + row],
            device_id=(q, target_row),
            device_id_type=MESH,
        )

    own_w = pltpu.make_async_copy(
        weight.at[pl.ds(pl.multiple_of(me * part, part), part)],
        gathered.at[
            me, row, :, pl.ds(pl.multiple_of(lax.rem(me, share) * w_cols, w_cols), w_cols)
        ],
        local_sem.at[0],
    )

    def start_scatter(i, carry):
        q = lax.rem(me + i, pools)
        scatter_copy(q).start()
        return carry

    lax.fori_loop(1, pools, start_scatter, 0)

    @pl.when(at_home)
    def _():
        own_w.start()

    @pl.when(jnp.logical_not(at_home))
    def _():
        scatter_copy(me).start()

    def start_kv(i, carry):
        q = lax.rem(me + i, pools)
        for r in range(cap):
            slot = meta_ref[q, r]
            send_k[q, r] = pool_k[slot]
            send_v[q, r] = pool_v[slot]
        for copy in kv_copies(q):
            copy.start()
        return carry

    lax.fori_loop(1, pools, start_kv, 0)
    for r in range(cap):
        slot = meta_ref[me, r]
        keys[me, r] = pool_k[slot]
        vals[me, r] = pool_v[slot]

    halves = 2
    half_rows = tps // halves

    def slab_copy(slab, half, pool_index, send_sem):
        piece = gathered.at[slab, pl.ds(half * half_rows, half_rows)]
        return pltpu.make_async_remote_copy(
            src_ref=piece,
            dst_ref=piece,
            send_sem=send_sem,
            recv_sem=g_recv.at[slab, half],
            device_id=(pool_index, row),
            device_id_type=MESH,
        )

    def chip_peer(i):
        return lax.rem(chip + i, chips) * 2 + core

    def chip_source(i):
        return lax.rem(chip + chips - i, chips) * 2 + core

    relay = chips == 4
    next_x = (chip + 1 - 2 * lax.rem(chip, 2)) * 2 + core
    next_y = lax.rem(chip + 2, 4) * 2 + core
    across = (lax.rem(chip + 2, 4) + 1 - 2 * lax.rem(chip, 2)) * 2 + core

    def own_slab_sends():
        if relay:
            order = [(next_x, 0), (next_y, 1), (next_x, 1), (next_y, 0)]
            return [(me, half, peer, g_send.at[n]) for n, (peer, half) in enumerate(order)]
        return []

    def relay_sends():
        return [(next_x, 0, next_y, g_send.at[4]), (next_y, 1, next_x, g_send.at[5])]

    def core_send(n, slab, half):
        return (slab, half, sibling, f_send.at[n, half])

    def start_gather():
        def wait_piece(i, carry):
            piece_pool = row * share + i // tps
            piece_row = lax.rem(i, tps)

            @pl.when(jnp.logical_not((piece_pool == me) & (piece_row == row)))
            def _():
                landing = gathered.at[
                    me,
                    piece_row,
                    :,
                    pl.ds(pl.multiple_of((i // tps) * w_cols, w_cols), w_cols),
                ]
                pltpu.make_async_remote_copy(
                    src_ref=landing,
                    dst_ref=landing,
                    send_sem=s_send.at[0],
                    recv_sem=s_recv.at[i],
                    device_id=(piece_pool, piece_row),
                    device_id_type=MESH,
                ).wait_recv()

            return carry

        lax.fori_loop(0, share * tps, wait_piece, 0)

        @pl.when(at_home)
        def _():
            own_w.wait()

        if relay:
            for item in own_slab_sends():
                slab_copy(*item).start()
        else:

            def start_slab(i, carry):
                for half in range(halves):
                    slab_copy(me, half, chip_peer(i), g_send.at[i * halves + half]).start()
                return carry

            lax.fori_loop(1, chips, start_slab, 0)
        for half in range(halves):
            slab_copy(*core_send(0, me, half)).start()

    def pass_on(n, slab, half, onward=None):
        to_core = slab_copy(*core_send(n, slab, half))
        to_core.wait_recv()
        if onward is not None:
            slab_copy(*onward).start()
        to_core.start()

    factor = math.log2(math.e) / math.sqrt(head)
    tables = []
    for e in range(seats):
        far, near = meta_ref[4 * pools + e, 0], meta_ref[4 * pools + e, 1]
        ca, sa = cos_far[pl.ds(far, 1), :], sin_far[pl.ds(far, 1), :]
        cb, sb = cos_near[pl.ds(near, 1), :], sin_near[pl.ds(near, 1), :]
        ca, sa = ca * cb - sa * sb, sa * cb + ca * sb
        cb, sb = cos_near[...], sin_near[...]
        tables.append((ca * cb - sa * sb, sa * cb + ca * sb))

    def rope(x, cosine, sine):
        return x * cosine + pltpu.roll(x, head // 2, 1) * sine

    lanes = lax.broadcasted_iota(jnp.int32, (turn, wide), 1)
    unseen = lax.broadcasted_iota(jnp.int32, (turn, wide), 0) > lax.rem(lanes, turn)
    for e in range(seats):
        cosine, sine = tables[e]
        rows = slice(e * turn, (e + 1) * turn)
        for h in range(group):
            x = tq_ref[rows, h * head : (h + 1) * head].astype(F32)
            turned = rope(x, cosine, sine) * factor
            queries[e * head : (e + 1) * head, h * turn : (h + 1) * turn] = turned.T.astype(BF16)
        new_keys = rope(tk_ref[rows, :].astype(F32), cosine, sine).astype(BF16)
        s = jnp.where(unseen, -jnp.inf, dot(new_keys, queries[e * head : (e + 1) * head, :]))
        best = jnp.max(s, axis=0, keepdims=True)
        p = jnp.exp2(s - best)
        top[e : e + 1, :] = best
        total[e : e + 1, :] = jnp.sum(p, axis=0, keepdims=True)
        flipped_new = tv_ref[rows, :].astype(F32).T.astype(BF16)
        acc[e * head : (e + 1) * head, :] = dot(flipped_new, p.astype(BF16))

    depth = lax.broadcasted_iota(jnp.int32, (block, 1), 0)

    def attend(source):
        tops = [top[e : e + 1, :] for e in range(seats)]
        owners = []
        for b in range(cap):
            far, seat = meta_ref[pools + source, b], meta_ref[2 * pools + source, b]
            owners.append(seat)
            ca, sa = cos_far[pl.ds(far, 1), :], sin_far[pl.ds(far, 1), :]
            cb, sb = cos_near[0:block, :], sin_near[0:block, :]
            x = keys[source, b].astype(F32)
            turned = rope(x, ca * cb - sa * sb, sa * cb + ca * sb)
            upright = vals[source, b].astype(F32).T
            span = slice(b * block, (b + 1) * block)
            for e in range(seats):
                part_e = slice(e * head, (e + 1) * head)
                wide_keys[span, part_e] = jnp.where(seat == e, turned, 0.0).astype(BF16)
                flipped[part_e, span] = jnp.where(seat == e, upright, 0.0).astype(BF16)
        run = math.gcd(cap, 4)
        for first in range(0, cap, run):
            several = dot(
                wide_keys[first * block : (first + run) * block, :], queries[...]
            )
            for b in range(first, first + run):
                s = several[(b - first) * block : (b - first + 1) * block, :]
                s = jnp.where(depth < meta_ref[3 * pools + source, b], s, -jnp.inf)
                scores[b * block : (b + 1) * block, :] = s
                best = jnp.max(s, axis=0, keepdims=True)
                for e in range(seats):
                    tops[e] = jnp.maximum(tops[e], jnp.where(owners[b] == e, best, -jnp.inf))
        alphas = [jnp.exp2(top[e : e + 1, :] - tops[e]) for e in range(seats)]
        sums = [total[e : e + 1, :] * alphas[e] for e in range(seats)]
        for b in range(cap):
            span = slice(b * block, (b + 1) * block)
            base = tops[0]
            for e in range(1, seats):
                base = jnp.where(owners[b] == e, tops[e], base)
            p = jnp.exp2(scores[span, :] - base)
            added = jnp.sum(p, axis=0, keepdims=True)
            for e in range(seats):
                sums[e] = sums[e] + jnp.where(owners[b] == e, added, 0.0)
            probs[span, :] = p.astype(BF16)
        gained = dot(flipped[...], probs[...])
        for e in range(seats):
            rows = slice(e * head, (e + 1) * head)
            acc[rows, :] = acc[rows, :] * alphas[e] + gained[rows, :]
            top[e : e + 1, :] = tops[e]
            total[e : e + 1, :] = sums[e]

    if relay:
        first, second = relay_sends()
        passes = [
            [(1, next_x, 0, first), (2, next_y, 1, second)],
            [(1, next_x, 1), (2, next_y, 0)],
            [(3, across, 0), (3, across, 1)],
        ]
    else:
        passes = []

    def step(i, carry):
        source = lax.rem(me + pools - i, pools)

        @pl.when(i > 0)
        def _():
            for copy in kv_arrival(source):
                copy.wait_recv()

        @pl.when(i == pools // 2 - 1)
        def _():
            start_gather()

        for n, items in enumerate(passes[:2]):

            @pl.when(i == pools - 2 + n)
            def _(items=items):
                for item in items:
                    pass_on(*item)

        attend(source)
        return carry

    lax.fori_loop(0, pools, step, 0)

    for e in range(seats):
        rows = slice(e * turn, (e + 1) * turn)
        final = acc[e * head : (e + 1) * head, :] / total[e : e + 1, :]
        for h in range(group):
            attended[row, rows, h * head : (h + 1) * head] = (
                final[:, h * turn : (h + 1) * turn].T.astype(BF16)
            )

    def slot_copy(slot, neighbour, way, hop):
        return pltpu.make_async_remote_copy(
            src_ref=attended.at[slot],
            dst_ref=attended.at[slot],
            send_sem=a_send.at[way, hop],
            recv_sem=a_recv.at[slot],
            device_id=(me, neighbour),
            device_id_type=MESH,
        )

    def hop_sends(hop, act):
        @pl.when((row - hop >= 0) & (row < tps - 1))
        def _():
            act(slot_copy(row - hop, row + 1, 0, hop))

        @pl.when((row + hop < tps) & (row > 0))
        def _():
            act(slot_copy(row + hop, row - 1, 1, hop))

    def hop_waits(hop):
        @pl.when(row - hop >= 0)
        def _():
            slot_copy(row - hop, row - 1, 0, 0).wait_recv()

        @pl.when(row + hop < tps)
        def _():
            slot_copy(row + hop, row + 1, 1, 0).wait_recv()

    hop_sends(0, lambda copy: copy.start())
    for items in passes[2:]:
        for item in items:
            pass_on(*item)
    if not relay:

        def rest(i, carry):
            for half in range(halves):
                pass_on(i, chip_source(i), half)
            return carry

        lax.fori_loop(1, chips, rest, 0)

    def wait_passed(i, carry):
        slab = chip_source(i) - core + lax.rem(sibling, 2)
        for half in range(halves):
            slab_copy(slab, half, sibling, g_send.at[0]).wait_recv()
        return carry

    lax.fori_loop(0, chips, wait_passed, 0)

    tile = 512
    tiles = out_ref.shape[1] // tile

    def project(slot, first):
        def one(c, carry):
            cols = pl.ds(pl.multiple_of(c * tile, tile), tile)
            w = gathered[:, slot, :, cols].reshape(pools * part, tile)
            result = dot(attended[slot], w)
            if not first:
                result = result + partial[:, cols]
            partial[:, cols] = result
            return carry

        lax.fori_loop(0, tiles, one, 0)

    project(row, True)
    for hop in range(1, tps):
        hop_waits(hop)
        if hop < tps - 1:
            hop_sends(hop, lambda copy: copy.start())

        @pl.when(row - hop >= 0)
        def _():
            project(row - hop, False)

        @pl.when(row + hop < tps)
        def _():
            project(row + hop, False)

    out_ref[...] = partial[...].astype(BF16)

    def wait_sends(i, carry):
        q = lax.rem(me + i, pools)
        for copy in kv_copies(q):
            copy.wait_send()
        scatter_copy(q).wait_send()
        return carry

    lax.fori_loop(1, pools, wait_sends, 0)

    @pl.when(jnp.logical_not(at_home))
    def _():
        scatter_copy(me).wait_send()

    if relay:
        for item in own_slab_sends() + relay_sends():
            slab_copy(*item).wait_send()
        for n, slab in enumerate((me, next_x, next_y, across)):
            for half in range(halves):
                slab_copy(*core_send(n, slab, half)).wait_send()
    else:

        def wait_slabs(i, carry):
            for half in range(halves):
                slab_copy(me, half, chip_peer(i), g_send.at[i * halves + half]).wait_send()
                slab_copy(*core_send(i, chip_source(i), half)).wait_send()
            return carry

        lax.fori_loop(1, chips, wait_slabs, 0)
        for half in range(halves):
            slab_copy(*core_send(0, me, half)).wait_send()
    for hop in range(tps - 1):
        hop_sends(hop, lambda copy: copy.wait_send())


def plan(pools, seats, cap, blocks_here, block, seat_ref, len_ref, map_ref, out_ref):
    me = lax.axis_index("pool")
    slots, block_count = map_ref.shape[0], map_ref.shape[1]
    seated = pools * seats

    def iota(shape, dim):
        return lax.broadcasted_iota(jnp.int32, shape, dim)

    def lane_sum(mask, x):
        return jnp.sum(jnp.where(mask, x, 0.0), axis=1, keepdims=True)

    sits = seat_ref[...] == iota((seated, slots), 1)
    lengths = lane_sum(sits, len_ref[...].astype(F32))
    all_slots = map_ref[...].astype(F32)
    seat_map = jnp.zeros((seated, block_count), F32)
    for session in range(slots):
        seat_map = seat_map + jnp.where(
            seat_ref[...] == session, all_slots[session : session + 1, :], 0.0
        )
    home = jnp.floor(seat_map * (1.0 / blocks_here))
    slot = seat_map - home * blocks_here
    numbers = iota((seated, block_count), 1).astype(F32)
    alive = numbers * block < lengths
    upto = jnp.where(
        iota((block_count, block_count), 0) <= iota((block_count, block_count), 1), 1.0, 0.0
    )

    leaving = alive & (home == me.astype(F32))
    flags = jnp.where(leaving, 1.0, 0.0)
    row_a, row_b = iota((seated, seated), 0), iota((seated, seated), 1)
    before = jnp.where((row_b < row_a) & (row_b // seats == row_a // seats), 1.0, 0.0)
    offset = jnp.sum(dot(before, flags), axis=1, keepdims=True)
    rank = dot(flags, upto) - 1.0 + offset
    merge = jnp.where(
        iota((pools, seated), 0) == iota((pools, seated), 1) // seats, 1.0, 0.0
    )
    for r in range(cap):
        picked = dot(merge, jnp.where(leaving & (rank == r), slot, 0.0))
        out_ref[0:pools, r : r + 1] = jnp.sum(picked, axis=1, keepdims=True).astype(jnp.int32)

    sources = iota((pools, block_count), 0).astype(F32)
    order = iota((pools, block_count), 1).astype(F32)
    taken = jnp.zeros((pools, 1), F32)
    found = [[jnp.zeros((pools, 1), F32) for r in range(cap)] for kind in range(3)]
    rows = iota((seated, block_count), 0)
    for e in range(seats):
        mine = rows == me * seats + e
        own_home = jnp.sum(jnp.where(mine, home, 0.0), axis=0, keepdims=True)
        own_length = jnp.sum(
            jnp.where(mine, lengths + jnp.zeros_like(home), 0.0), axis=0, keepdims=True
        )
        coming = (order * block < own_length) & (own_home == sources)
        flags = jnp.where(coming, 1.0, 0.0)
        rank = dot(flags, upto) - 1.0 + taken
        taken = taken + jnp.sum(flags, axis=1, keepdims=True)
        for r in range(cap):
            hit = coming & (rank == r)
            found[0][r] = found[0][r] + lane_sum(hit, order)
            found[1][r] = found[1][r] + lane_sum(hit, jnp.full_like(order, e + 1.0))
            found[2][r] = found[2][r] + lane_sum(hit, own_length - order * block)
        length = own_length[:, 0:1]
        far = jnp.floor(length * (1.0 / block))
        out_ref[4 * pools + e : 4 * pools + e + 1, 0:1] = far.astype(jnp.int32)
        out_ref[4 * pools + e : 4 * pools + e + 1, 1:2] = (length - far * block).astype(jnp.int32)
    for kind in range(3):
        for r in range(cap):
            value = found[kind][r] - (1.0 if kind == 1 else 0.0)
            out_ref[(kind + 1) * pools : (kind + 2) * pools, r : r + 1] = value.astype(jnp.int32)


def local(
    turn_query,
    turn_key,
    turn_value,
    pool_keys,
    pool_values,
    seat_session,
    history_len,
    block_map,
    out_weight,
):
    pools = lax.axis_size("pool")
    tps = lax.axis_size("tp")
    block, head = pool_keys.shape[1:]
    block_count = block_map.shape[1]
    seats = seat_session.shape[0] // pools
    cap = seats * block_count // pools
    rows, width = turn_query.shape
    turn = rows // seats
    group = width // head
    wide = group * turn
    part = out_weight.shape[0] // pools
    out_cols = out_weight.shape[1] * pools // tps

    in_vmem = pl.BlockSpec(memory_space=pltpu.VMEM)
    in_smem = pl.BlockSpec(memory_space=pltpu.SMEM)
    anywhere = pl.BlockSpec(memory_space=pl.ANY)
    dma = pltpu.SemaphoreType.DMA

    meta = pl.pallas_call(
        functools.partial(plan, pools, seats, cap, pool_keys.shape[0], block),
        out_shape=jax.ShapeDtypeStruct((4 * pools + 8, max(cap, 2)), jnp.int32),
        in_specs=[in_vmem] * 3,
        out_specs=in_vmem,
    )(seat_session[:, None], history_len[None, :], block_map)

    half = head // 2
    inverse = rope_base ** (-2.0 * np.arange(half) / head)
    inverse = np.concatenate([inverse, inverse])
    signs = np.concatenate([-np.ones(half), np.ones(half)])
    near = np.arange(turn)[:, None] * inverse[None, :]
    far = (np.arange(block_count + 1) * block)[:, None] * inverse[None, :]
    cos_near = jnp.asarray(np.cos(near), F32)
    sin_near = jnp.asarray(np.sin(near) * signs, F32)
    cos_far = jnp.asarray(np.cos(far), F32)
    sin_far = jnp.asarray(np.sin(far) * signs, F32)

    chips = pools // 2
    return pl.pallas_call(
        functools.partial(kernel, pools, tps, seats, cap),
        out_shape=jax.ShapeDtypeStruct((rows, out_cols), BF16),
        in_specs=[in_smem] + [in_vmem] * 9 + [anywhere],
        out_specs=in_vmem,
        scratch_shapes=[
            pltpu.VMEM((pools, cap, block, head), BF16),
            pltpu.VMEM((pools, cap, block, head), BF16),
            pltpu.VMEM((pools, cap, block, head), BF16),
            pltpu.VMEM((pools, cap, block, head), BF16),
            pltpu.VMEM((pools, tps, part, out_cols), BF16),
            pltpu.VMEM((tps, rows, width), BF16),
            pltpu.VMEM((seats * head, wide), BF16),
            pltpu.VMEM((cap * block, seats * head), BF16),
            pltpu.VMEM((cap * block, wide), F32),
            pltpu.VMEM((cap * block, wide), BF16),
            pltpu.VMEM((seats * head, cap * block), BF16),
            pltpu.VMEM((seats * head, wide), F32),
            pltpu.VMEM((seats, wide), F32),
            pltpu.VMEM((seats, wide), F32),
            pltpu.VMEM((rows, out_cols), F32),
            dma((pools,)),
            dma((pools,)),
            dma((pools,)),
            dma((pools,)),
            dma((pools,)),
            dma((pools,)),
            dma((2 * chips,)),
            dma((pools, 2)),
            dma((chips, 2)),
            dma((2, tps)),
            dma((tps,)),
            dma((1,)),
        ],
        compiler_params=pltpu.CompilerParams(
            collective_id=0, has_side_effects=True, vmem_limit_bytes=56 * 1024 * 1024
        ),
    )(
        meta,
        turn_query,
        turn_key,
        turn_value,
        cos_far,
        sin_far,
        cos_near,
        sin_near,
        pool_keys,
        pool_values,
        out_weight,
    )


def solution(mesh):
    return jax.shard_map(
        local,
        mesh=mesh,
        in_specs=(
            P("pool", "tp"),
            P("pool", "tp"),
            P("pool", "tp"),
            P("pool", None, "tp"),
            P("pool", None, "tp"),
            P(),
            P(),
            P(),
            P("tp", "pool"),
        ),
        out_specs=P("pool", "tp"),
        check_vma=False,
    )
```
